32 devices in a mesh: seq: 16 (over z, x, core), mp: 2 (over y).
Axes of the slice: x: 2, y: 2, z: 4, core: 2. Of those that a mesh axis runs over, the one named last changes fastest.
Arguments:
- queries: bfloat16 [2048, 2048], P('seq', 'mp'), may hold values from -200 to 200
- keys: bfloat16 [2048, 256], P('seq', 'mp'), may hold values from -7 to 7
- values: float32 [2048, 256], P('seq', 'mp'), may hold values from -24 to 24
- inputs_x: bfloat16 [2048, 2048], P('seq', 'mp'), may hold values from -6 to 6
- in_b: bfloat16 [2048, 128], P('seq'), may hold values from -6 to 6
- in_c: bfloat16 [2048, 128], P('seq'), may hold values from -6 to 6
- log_decay: float32 [2048, 16], P('seq', 'mp'), may hold values from -2 to 0
Outputs:
- grad_x: float32 [2048, 2048], P('seq', 'mp')
- grad_b: float32 [2048, 128], P(('seq', 'mp'))
- grad_c: float32 [2048, 128], P(('seq', 'mp'))
The draws below stay inside these ranges and needn't reach their ends.
All inputs are finite; a program needn't handle non-finite values.
Results may differ from the reference program's by a relative error of at most 0.00035.
Values may be sent and summed in bfloat16 or wider, within the bound.
A program may use at most 128 MiB of HBM per device.

```python
import math
from functools import partial
import jax
import jax.numpy as jnp
from jax import lax

SHARD_TOKENS = 128
HEAD_WIDTH = 128
N = 128
QUERY_HEADS = 16
KEY_VALUE_HEADS = 2
TOKEN_COUNT = 2048
N_SEQ = 16


def drawn(key):
    base_key_index = jnp.clip(jax.random.normal(jax.random.fold_in(key, 11), (TOKEN_COUNT, KEY_VALUE_HEADS * HEAD_WIDTH), jnp.float32), -6.0, 6.0)
    base_q = 2.0 * jnp.clip(jax.random.normal(jax.random.fold_in(key, 12), (TOKEN_COUNT, QUERY_HEADS * HEAD_WIDTH), jnp.float32), -6.0, 6.0)
    return (base_q, base_key_index)


def draw_queries(key, part):
    return drawn(key)[0].astype(jnp.bfloat16)


def draw_keys(key, part):
    return drawn(key)[1].astype(jnp.bfloat16)


def draw_log_decay(key, part):
    fast_share = 0.5
    fast_heads = jax.random.uniform(jax.random.fold_in(key, 21), (QUERY_HEADS,), jnp.float32) < fast_share
    fast_rate = jax.random.uniform(jax.random.fold_in(key, 22), (QUERY_HEADS,), jnp.float32, 1.0 / 50.0, 1.0 / 30.0)
    slow_total = jnp.exp(jax.random.uniform(jax.random.fold_in(key, 23), (QUERY_HEADS,), jnp.float32, math.log(0.1), math.log(0.3)))
    base_rate = jnp.where(fast_heads, fast_rate, slow_total / TOKEN_COUNT)
    token_factor = jax.random.uniform(jax.random.fold_in(key, 24), (TOKEN_COUNT, QUERY_HEADS), jnp.float32, 0.5, 1.5)
    block_factor = jnp.exp(jax.random.uniform(jax.random.fold_in(key, 25), (TOKEN_COUNT // SHARD_TOKENS, 1, QUERY_HEADS), jnp.float32, math.log(0.5), math.log(2.0)))
    block_factor = jnp.broadcast_to(block_factor, (TOKEN_COUNT // SHARD_TOKENS, SHARD_TOKENS, QUERY_HEADS)).reshape(TOKEN_COUNT, QUERY_HEADS)
    stable_state = -base_rate[None, :] * token_factor * block_factor
    cluster_rows = jax.random.randint(jax.random.fold_in(key, 26), (3, QUERY_HEADS), 0, TOKEN_COUNT)
    cluster_size = jax.random.uniform(jax.random.fold_in(key, 27), (3, QUERY_HEADS), jnp.float32, 0.22, 0.5)
    head_index_list = jnp.broadcast_to(jnp.arange(QUERY_HEADS, dtype=jnp.int32)[None, :], (3, QUERY_HEADS))
    cluster_list = jnp.zeros((TOKEN_COUNT, QUERY_HEADS), jnp.float32).at[cluster_rows, head_index_list].add(-cluster_size)
    return stable_state + cluster_list


def steps_of(key, shape, cuts, low, top_value):
    factor_of, own = 1.0, jax.random.fold_in(key, 6)
    for dim, blocks in cuts:
        draws = jnp.exp(jax.random.uniform(jax.random.fold_in(own, dim), (blocks,), jnp.float32, low / len(cuts), top_value / len(cuts)))
        factor_of = factor_of * jnp.repeat(draws, shape[dim] // blocks).reshape([-1 if axis == dim else 1 for axis in range(len(shape))])
    return factor_of


def normal_values(stream_key, extent, spread, limit, pieces=(), kind=jnp.bfloat16):
    entries = spread * jax.random.normal(stream_key, extent, jnp.float32)
    if pieces:
        entries = entries * steps_of(stream_key, extent, pieces, -0.22, 0.18)
    return jnp.clip(entries, -limit, limit).astype(kind)


def setup_inputs(seed: int = 0) -> dict:
    streams_of = jax.random.split(jax.random.key(seed), 8)
    queries = draw_queries(jax.random.fold_in(streams_of[7], 71), 0)
    keys = draw_keys(jax.random.fold_in(streams_of[7], 71), 0)
    values = normal_values(streams_of[2], (TOKEN_COUNT, KEY_VALUE_HEADS * HEAD_WIDTH), 4.0, 24.0, ((0, 16), (1, 2)), jnp.float32)
    inputs_x = normal_values(streams_of[3], (TOKEN_COUNT, QUERY_HEADS * HEAD_WIDTH), 1.0, 6.0, ((0, 16), (1, 2)))
    in_b = normal_values(streams_of[4], (TOKEN_COUNT, N), 1.0, 6.0, ((0, 16),))
    in_c = normal_values(streams_of[5], (TOKEN_COUNT, N), 1.0, 6.0, ((0, 16),))
    log_decay = draw_log_decay(jax.random.fold_in(streams_of[7], 71), 0)
    return dict(queries=queries, keys=keys, values=values, inputs_x=inputs_x, in_b=in_b, in_c=in_c, log_decay=log_decay)


very_negative = -1e+30
highest = lax.Precision.HIGHEST

def teacher_block(block_data, every_key, every_value):
    query_tile_block, block_start = block_data
    group_width = QUERY_HEADS // KEY_VALUE_HEADS
    query_head_rows = query_tile_block.reshape(SHARD_TOKENS, KEY_VALUE_HEADS, group_width, HEAD_WIDTH).astype(jnp.float32)
    key_head_rows = every_key.reshape(TOKEN_COUNT, KEY_VALUE_HEADS, HEAD_WIDTH).astype(jnp.float32)
    value_head_rows = every_value.reshape(TOKEN_COUNT, KEY_VALUE_HEADS, HEAD_WIDTH).astype(jnp.float32)
    scores = jnp.einsum('qkgd,nkd->qkgn', query_head_rows, key_head_rows, precision=highest) / math.sqrt(HEAD_WIDTH)
    query_pos = block_start + jnp.arange(SHARD_TOKENS, dtype=jnp.int32)
    key_pos = jnp.arange(TOKEN_COUNT, dtype=jnp.int32)
    allowed = (key_pos[None, :] <= query_pos[:, None])[:, None, None, :]
    scores = jnp.where(allowed, scores, very_negative)
    row_top = lax.optimization_barrier(jnp.max(scores, axis=-1, keepdims=True))
    weights = jnp.where(allowed, jnp.exp(scores - row_top), 0.0)
    denominator = lax.optimization_barrier(jnp.sum(weights, axis=-1))
    mixture = jnp.einsum('qkgn,nkd->qkgd', weights, value_head_rows, precision=highest)
    return (mixture / denominator[..., None]).reshape(SHARD_TOKENS, QUERY_HEADS, HEAD_WIDTH)

def decay_matrix(cumulative):
    heads_first = cumulative.T
    causal = jnp.arange(SHARD_TOKENS)[:, None] >= jnp.arange(SHARD_TOKENS)[None, :]
    log_gaps = jnp.where(causal[None], heads_first[:, :, None] - heads_first[:, None, :], -jnp.inf)
    return jnp.exp(log_gaps)

def span_forward(state_in, span_data):
    student_x, b_rows, c_rows, step_logs = span_data
    cumulative = jnp.cumsum(step_logs, axis=0)
    totals = cumulative[-1]
    decays = decay_matrix(cumulative)
    inner_products = jnp.dot(c_rows, b_rows.T, precision=highest)
    mixing = decays * inner_products[None]
    y_intra = jnp.einsum('hts,shp->thp', mixing, student_x, precision=highest)
    rising = jnp.exp(cumulative)
    y_inter = jnp.einsum('tn,hpn->thp', c_rows, state_in, precision=highest) * rising[:, :, None]
    ending = jnp.exp(totals[None, :] - cumulative)
    local_state = jnp.einsum('shp,sn->hpn', student_x * ending[:, :, None], b_rows, precision=highest)
    state_out = jnp.exp(totals)[:, None, None] * state_in + local_state
    return (state_out, (y_intra + y_inter, state_in))

def span_backward(later_grad, span_data):
    student_x, b_rows, c_rows, step_logs, mismatch, state_in = span_data
    cumulative = jnp.cumsum(step_logs, axis=0)
    totals = cumulative[-1]
    decays = decay_matrix(cumulative)
    inner_products = jnp.dot(c_rows, b_rows.T, precision=highest)
    mixing = decays * inner_products[None]
    rising = jnp.exp(cumulative)
    ending = jnp.exp(totals[None, :] - cumulative)
    grad_x = jnp.einsum('hts,thp->shp', mixing, mismatch, precision=highest)
    grad_x = grad_x + jnp.einsum('hpn,sn->shp', later_grad, b_rows, precision=highest) * ending[:, :, None]
    products = jnp.einsum('thp,shp->hts', mismatch, student_x, precision=highest)
    weighted = decays * products
    grad_b = jnp.einsum('hts,tn->sn', weighted, c_rows, precision=highest)
    grad_b = grad_b + jnp.einsum('shp,hpn->sn', student_x * ending[:, :, None], later_grad, precision=highest)
    grad_c = jnp.einsum('hts,sn->tn', weighted, b_rows, precision=highest)
    grad_c = grad_c + jnp.einsum('thp,hpn->tn', mismatch * rising[:, :, None], state_in, precision=highest)
    local_grad = jnp.einsum('thp,tn->hpn', mismatch * rising[:, :, None], c_rows, precision=highest)
    earlier_grad = local_grad + jnp.exp(totals)[:, None, None] * later_grad
    return (earlier_grad, (grad_x, grad_b, grad_c))

def reference(queries, keys, values, inputs_x, in_b, in_c, log_decay):
    starts = jnp.arange(N_SEQ, dtype=jnp.int32) * SHARD_TOKENS
    teacher_out = lax.map(partial(teacher_block, every_key=keys, every_value=values), (queries.reshape(N_SEQ, SHARD_TOKENS, QUERY_HEADS * HEAD_WIDTH), starts))
    c_scale = 0.5 / math.sqrt(N * TOKEN_COUNT)
    student_x = inputs_x.astype(jnp.float32).reshape(N_SEQ, SHARD_TOKENS, QUERY_HEADS, HEAD_WIDTH)
    b_rows = in_b.astype(jnp.float32).reshape(N_SEQ, SHARD_TOKENS, N)
    c_rows = (in_c.astype(jnp.float32) * c_scale).reshape(N_SEQ, SHARD_TOKENS, N)
    step_logs = log_decay.reshape(N_SEQ, SHARD_TOKENS, QUERY_HEADS)
    start_state = jnp.zeros((QUERY_HEADS, HEAD_WIDTH, N), jnp.float32)
    unused_state, (student_out, states_in) = lax.scan(span_forward, start_state, (student_x, b_rows, c_rows, step_logs))
    mismatch = student_out - teacher_out
    unused_grad, (grad_x, grad_b, grad_c) = lax.scan(span_backward, start_state, (student_x, b_rows, c_rows, step_logs, mismatch, states_in), reverse=True)
    return (grad_x.reshape(TOKEN_COUNT, QUERY_HEADS * HEAD_WIDTH), grad_b.reshape(TOKEN_COUNT, N), grad_c.reshape(TOKEN_COUNT, N) * c_scale)
```

```python
import functools
import math

import jax
import jax.numpy as jnp
from jax import lax
from jax.experimental import pallas as pl
from jax.experimental.pallas import tpu as pltpu
from jax.sharding import PartitionSpec as P

W = 128
HEADS = 8
PLANE = 4
MESH = pl.DeviceIdType.MESH
F32 = jnp.float32
BF = jnp.bfloat16
LOW = -1e30


def dot(a, b):
    return lax.dot_general(a, b, (((1,), (0,)), ((), ())), preferred_element_type=F32)


def dot_nt(a, b):
    return lax.dot_general(a, b, (((1,), (1,)), ((), ())), preferred_element_type=F32)


def split(v):
    hi = v.astype(BF)
    return hi, (v - hi.astype(F32)).astype(BF)


def kernel(
    planes, mp, c_scale,
    q_ref, k_ref, v_ref, x_ref, b_ref, c_ref, ld_ref,
    gx_ref, gb_ref, gc_ref,
    kv, cum, lsend, rs, zin, zout, ag_out, s_in,
    lgsend, rsb, zinb, zoutb, agb_out, g_in,
    decay, mixt, ybuf, acc, top, den, qs, dbuf, gsum, mpb,
    kv_r, col_s, x_s, core_s, diag_s,
    rs_s, rs_r, z_s, z_r, ag_s, ag_r,
    rsb_s, rsb_r, zb_s, zb_r, agb_s, agb_r,
    mp_s, mp_r,
):
    s = lax.axis_index("seq")
    m = lax.axis_index("mp")
    z = s // PLANE
    r = s % PLANE
    base = z * PLANE
    core = r % 2
    rx = (r + 2) % PLANE
    rc = r + 1 - 2 * core
    rd = (rc + 2) % PLANE
    up = lax.rem(s + PLANE, planes * PLANE)
    down = lax.rem(s + (planes - 1) * PLANE, planes * PLANE)
    not_last = z < planes - 1
    not_first = z > 0
    rows = W // mp

    barrier = pltpu.get_barrier_semaphore()
    for k in range(1, PLANE):
        pl.semaphore_signal(
            barrier, inc=1, device_id=(base + (r + k) % PLANE, m), device_id_type=MESH
        )
    for k in range(1, mp):
        pl.semaphore_signal(barrier, inc=1, device_id=(s, (m + k) % mp), device_id_type=MESH)

    @pl.when(not_last)
    def _():
        pl.semaphore_signal(barrier, inc=1, device_id=(up, m), device_id_type=MESH)

    @pl.when(not_first)
    def _():
        pl.semaphore_signal(barrier, inc=1, device_id=(down, m), device_id_type=MESH)

    v_hi, v_lo = split(v_ref[...])
    kv[z, r, :, 0:W] = k_ref[...]
    kv[z, r, :, W : 2 * W] = v_hi
    kv[z, r, :, 2 * W : 3 * W] = v_lo

    extra = jnp.where(not_last, 1, 0) + jnp.where(not_first, 1, 0)
    pl.semaphore_wait(barrier, PLANE - 1 + mp - 1 + extra)

    def remote(src, dst, send, recv, to):
        return pltpu.make_async_remote_copy(
            src_ref=src, dst_ref=dst, send_sem=send, recv_sem=recv,
            device_id=to, device_id_type=MESH,
        )

    def kv_copy(zp, rr, send, to):
        return remote(kv.at[zp, rr], kv.at[zp, rr], send.at[zp], kv_r.at[zp, rr], to)

    def col(zp):
        return kv_copy(zp, r, col_s, (up, m))

    def across(zp):
        return kv_copy(zp, r, x_s, (base + rx, m))

    def chip(zp):
        return kv_copy(zp, r, core_s, (base + rc, m))

    def diag(zp):
        return kv_copy(zp, rx, diag_s, (base + rc, m))

    def arrived(zp, rr):
        kv_copy(zp, rr, col_s, (base + rc, m)).wait_recv()

    def spread(zp):
        @pl.when(not_last)
        def _():
            col(zp).start()

        across(zp).start()
        chip(zp).start()

    spread(z)

    at_row = lax.broadcasted_iota(jnp.int32, (W, W), 0)
    at_col = lax.broadcasted_iota(jnp.int32, (W, W), 1)
    tri = jnp.where(at_row >= at_col, 1.0, 0.0).astype(BF)
    ld = ld_ref[...]
    for h in range(HEADS):
        wide = jnp.broadcast_to(ld[:, h : h + 1], (W, W))
        p0 = wide.astype(BF)
        rest = wide - p0.astype(F32)
        p1 = rest.astype(BF)
        p2 = (rest - p1.astype(F32)).astype(BF)
        cum[h] = dot(tri, p0) + dot(tri, p1) + dot(tri, p2)

    b = b_ref[...]
    c = c_ref[...]
    b_t = b.astype(F32).T.astype(BF)
    c_t = c.astype(F32).T.astype(BF)

    def head(ref, h):
        return ref[:, h * W : (h + 1) * W]

    for o in range(PLANE):
        for g in range(2):
            h = 2 * o + g
            total = cum[h, W - 1 : W, :]
            ending = jnp.exp(total - cum[h])
            hi, lo = split(head(x_ref, h).astype(F32) * ending)
            lsend[o, g, 0:W, :] = dot(b_t, hi) + dot(b_t, lo)
            lsend[o, g, W : W + 8, :] = jnp.broadcast_to(total, (8, W))

    def rs_copy(k):
        o = (r + k) % PLANE
        return remote(lsend.at[o], rs.at[r], rs_s.at[k], rs_r.at[r], (base + o, m))

    def rs_arrive(k):
        o = (r + k) % PLANE
        return remote(lsend.at[o], rs.at[o], rs_s.at[k], rs_r.at[o], (base + o, m))

    for k in range(1, PLANE):
        rs_copy(k).start()
    rs[r] = lsend[r]

    cb = dot_nt(c, b) * c_scale
    cb_t = dot_nt(b, c) * c_scale
    for h in range(HEADS):
        here = cum[h]
        other = here.T
        dec = jnp.exp(jnp.where(at_row >= at_col, here - other, LOW))
        dec_t = jnp.exp(jnp.where(at_row <= at_col, other - here, LOW))
        decay[h] = dec
        hi, lo = split(dec_t * cb_t)
        mixt[0, h] = hi
        mixt[1, h] = lo
        hi, lo = split(dec * cb)
        xh = head(x_ref, h)
        ybuf[h] = dot(hi, xh) + dot(lo, xh)
        qs[h] = head(q_ref, h)

    def forward_piece(i, carry):
        zp = z - 1 - i
        arrived(zp, r)
        spread(zp)
        return carry

    lax.fori_loop(0, z, forward_piece, 0)

    def plane_ready(zp):
        arrived(zp, rx)
        diag(zp).start()
        arrived(zp, rc)
        arrived(zp, rd)

    factor = math.log2(math.e) / math.sqrt(W)

    def attend(zp, first):
        keys = kv[zp, :, :, 0:W].reshape(PLANE * W, W)
        both = kv[zp, :, :, W : 3 * W].reshape(PLANE * W, 2 * W)
        v_top = kv[zp, :, :, W : 2 * W].reshape(PLANE * W, W)
        for h in range(HEADS):
            sc = dot_nt(qs[h], keys) * factor
            if first:
                t = lax.broadcasted_iota(jnp.int32, (W, PLANE * W), 0) + r * W
                u = lax.broadcasted_iota(jnp.int32, (W, PLANE * W), 1)
                sc = jnp.where(u <= t, sc, LOW)
            new = jnp.max(sc, axis=-1, keepdims=True)
            if not first:
                old = top[h][:, 0:1]
                new = jnp.maximum(old, new)
                scale = jnp.exp2(old - new)
            wt = jnp.exp2(sc - new)
            total = jnp.sum(wt, axis=-1, keepdims=True)
            hi, lo = split(wt)
            res = dot(hi, both)
            mix = res[:, 0:W] + res[:, W:] + dot(lo, v_top)
            if first:
                acc[h] = mix
                den[h] = jnp.broadcast_to(total, (W, W))
            else:
                acc[h] = acc[h] * scale + mix
                den[h] = den[h] * scale + total
            top[h] = jnp.broadcast_to(new, (W, W))

    plane_ready(z)
    attend(z, True)

    def attend_earlier(i, carry):
        zp = z - 1 - i
        plane_ready(zp)
        attend(zp, False)
        return carry

    def z_copy(g):
        return remote(zout.at[g], zin.at[g], z_s.at[g], z_r.at[g], (up, m))

    def ag_copy(k, g):
        o = (r + k) % PLANE
        return remote(
            ag_out.at[o, g], s_in.at[r, g], ag_s.at[k, g], ag_r.at[r, g], (base + o, m)
        )

    def ag_arrive(k, g):
        o = (r + k) % PLANE
        return remote(
            ag_out.at[o, g], s_in.at[o, g], ag_s.at[k, g], ag_r.at[o, g], (base + o, m)
        )

    before = jnp.where(not_last, 0, z)
    lax.fori_loop(0, before, attend_earlier, 0)

    for k in range(1, PLANE):
        rs_arrive(k).wait_recv()

    for g in range(2):
        pres, coefs = [None], [None]
        pre, coef = None, None
        for j in range(PLANE):
            e = jnp.exp(rs[j, g, W : W + 1, :])
            local = rs[j, g, 0:W, :]
            pre = local if pre is None else e * pre + local
            coef = e if coef is None else coef * e
            pres.append(pre)
            coefs.append(coef)

        @pl.when(not_first)
        def _():
            z_copy(g).wait_recv()

        @pl.when(jnp.logical_not(not_first))
        def _():
            zin[g] = jnp.zeros((W, W), F32)

        came = zin[g]
        zout[g] = coefs[PLANE] * came + pres[PLANE]

        @pl.when(not_last)
        def _():
            z_copy(g).start()

        for j in range(PLANE):
            ag_out[j, g] = came if j == 0 else coefs[j] * came + pres[j]
        for k in range(1, PLANE):
            ag_copy(k, g).start()
        s_in[r, g] = ag_out[r, g]

    lax.fori_loop(before, z, attend_earlier, 0)

    for k in range(1, PLANE):
        for g in range(2):
            ag_arrive(k, g).wait_recv()

    for o in range(PLANE):
        for g in range(2):
            h = 2 * o + g
            rising = jnp.exp(cum[h])
            hi, lo = split(s_in[o, g])
            inter = (dot(c, hi) + dot(c, lo)) * (rising * c_scale)
            d = ybuf[h] + inter - acc[h] / den[h]
            dbuf[h] = d
            hi, lo = split(d * rising)
            lgsend[o, g] = (dot(c_t, hi) + dot(c_t, lo)) * c_scale

    def rsb_copy(k):
        o = (r + k) % PLANE
        return remote(lgsend.at[o], rsb.at[r], rsb_s.at[k], rsb_r.at[r], (base + o, m))

    def rsb_arrive(k):
        o = (r + k) % PLANE
        return remote(lgsend.at[o], rsb.at[o], rsb_s.at[k], rsb_r.at[o], (base + o, m))

    for k in range(1, PLANE):
        rsb_copy(k).start()
    rsb[r] = lgsend[r]

    weighted = jnp.zeros((W, W), F32)
    grad_c = jnp.zeros((W, W), F32)
    for h in range(HEADS):
        d_hi, d_lo = split(dbuf[h])
        xh = head(x_ref, h)
        weighted += decay[h] * (dot_nt(d_hi, xh) + dot_nt(d_lo, xh))
        s_hi, s_lo = split(s_in[h // 2, h % 2])
        inter = dot_nt(d_hi, s_hi) + dot_nt(d_hi, s_lo) + dot_nt(d_lo, s_hi)
        grad_c += jnp.exp(cum[h]) * inter
        gx_ref[:, h * W : (h + 1) * W] = (
            dot(mixt[0, h], d_hi) + dot(mixt[0, h], d_lo) + dot(mixt[1, h], d_hi)
        )
    hi, lo = split(weighted)
    grad_c = (grad_c + dot(hi, b) + dot(lo, b)) * c_scale
    hi, lo = split(weighted.T)
    gsum[0] = (dot(hi, c) + dot(lo, c)) * c_scale
    gsum[1] = grad_c

    def mp_copy(k, which):
        to = (m + k) % mp
        return remote(
            gsum.at[which, pl.ds(pl.multiple_of(to * rows, 8), rows)],
            mpb.at[k - 1, which],
            mp_s.at[k - 1, which], mp_r.at[k - 1, which], (s, to),
        )

    for k in range(1, mp):
        mp_copy(k, 1).start()

    def zb_copy(g):
        return remote(zoutb.at[g], zinb.at[g], zb_s.at[g], zb_r.at[g], (down, m))

    def agb_copy(k, g):
        o = (r + k) % PLANE
        return remote(
            agb_out.at[o, g], g_in.at[r, g], agb_s.at[k, g], agb_r.at[r, g], (base + o, m)
        )

    def agb_arrive(k, g):
        o = (r + k) % PLANE
        return remote(
            agb_out.at[o, g], g_in.at[o, g], agb_s.at[k, g], agb_r.at[o, g], (base + o, m)
        )

    for k in range(1, PLANE):
        rsb_arrive(k).wait_recv()

    for g in range(2):
        sufs, coefs = {PLANE - 1: None}, {PLANE - 1: None}
        suf, coef = None, None
        for j in range(PLANE - 1, -1, -1):
            e = jnp.exp(rs[j, g, W : W + 1, :])
            local = rsb[j, g]
            suf = local if suf is None else e * suf + local
            coef = e if coef is None else coef * e
            sufs[j - 1] = suf
            coefs[j - 1] = coef

        @pl.when(not_last)
        def _():
            zb_copy(g).wait_recv()

        @pl.when(jnp.logical_not(not_last))
        def _():
            zinb[g] = jnp.zeros((W, W), F32)

        came = zinb[g]
        zoutb[g] = coefs[-1] * came + sufs[-1]

        @pl.when(not_first)
        def _():
            zb_copy(g).start()

        for j in range(PLANE):
            agb_out[j, g] = came if j == PLANE - 1 else coefs[j] * came + sufs[j]
        for k in range(1, PLANE):
            agb_copy(k, g).start()
        g_in[r, g] = agb_out[r, g]

    for k in range(1, PLANE):
        for g in range(2):
            agb_arrive(k, g).wait_recv()

    grad_b = gsum[0]
    for o in range(PLANE):
        for g in range(2):
            h = 2 * o + g
            ending = jnp.exp(cum[h, W - 1 : W, :] - cum[h])
            hi, lo = split(g_in[o, g])
            gx_ref[:, h * W : (h + 1) * W] += (dot(b, hi) + dot(b, lo)) * ending
            xh = head(x_ref, h)
            grad_b += (dot_nt(xh, hi) + dot_nt(xh, lo)) * ending
    gsum[0] = grad_b
    for k in range(1, mp):
        mp_copy(k, 0).start()

    for k in range(1, PLANE):
        rs_copy(k).wait_send()
        rsb_copy(k).wait_send()
        for g in range(2):
            ag_copy(k, g).wait_send()
            agb_copy(k, g).wait_send()

    def sent(zp, carry):
        @pl.when(not_last)
        def _():
            col(zp).wait_send()

        across(zp).wait_send()
        chip(zp).wait_send()
        diag(zp).wait_send()
        return carry

    lax.fori_loop(0, z + 1, sent, 0)

    @pl.when(not_last)
    def _():
        for g in range(2):
            z_copy(g).wait_send()

    @pl.when(not_first)
    def _():
        for g in range(2):
            zb_copy(g).wait_send()

    own = pl.ds(pl.multiple_of(m * rows, 8), rows)
    for which, out in ((1, gc_ref), (0, gb_ref)):
        total = gsum[which, own]
        for k in range(1, mp):
            mp_copy(k, which).wait_recv()
            total += mpb[k - 1, which]
        out[...] = total
    for which in range(2):
        for k in range(1, mp):
            mp_copy(k, which).wait_send()


def local(queries, keys, values, inputs_x, in_b, in_c, log_decay):
    tokens = queries.shape[0]
    seq = lax.axis_size("seq")
    mp = lax.axis_size("mp")
    planes = seq // PLANE
    c_scale = 0.5 / math.sqrt(W * tokens * seq)
    dma = pltpu.SemaphoreType.DMA
    scratch = [
        pltpu.VMEM((planes, PLANE, W, 3 * W), BF),
        pltpu.VMEM((HEADS, W, W), F32),
        pltpu.VMEM((PLANE, 2, W + 8, W), F32),
        pltpu.VMEM((PLANE, 2, W + 8, W), F32),
        pltpu.VMEM((2, W, W), F32),
        pltpu.VMEM((2, W, W), F32),
        pltpu.VMEM((PLANE, 2, W, W), F32),
        pltpu.VMEM((PLANE, 2, W, W), F32),
        pltpu.VMEM((PLANE, 2, W, W), F32),
        pltpu.VMEM((PLANE, 2, W, W), F32),
        pltpu.VMEM((2, W, W), F32),
        pltpu.VMEM((2, W, W), F32),
        pltpu.VMEM((PLANE, 2, W, W), F32),
        pltpu.VMEM((PLANE, 2, W, W), F32),
        pltpu.VMEM((HEADS, W, W), F32),
        pltpu.VMEM((2, HEADS, W, W), BF),
        pltpu.VMEM((HEADS, W, W), F32),
        pltpu.VMEM((HEADS, W, W), F32),
        pltpu.VMEM((HEADS, W, W), F32),
        pltpu.VMEM((HEADS, W, W), F32),
        pltpu.VMEM((HEADS, W, W), BF),
        pltpu.VMEM((HEADS, W, W), F32),
        pltpu.VMEM((2, W, W), F32),
        pltpu.VMEM((max(mp - 1, 1), 2, W // mp, W), F32),
        dma((planes, PLANE)), dma((planes,)), dma((planes,)), dma((planes,)), dma((planes,)),
        dma((PLANE,)), dma((PLANE,)), dma((2,)), dma((2,)), dma((PLANE, 2)), dma((PLANE, 2)),
        dma((PLANE,)), dma((PLANE,)), dma((2,)), dma((2,)), dma((PLANE, 2)), dma((PLANE, 2)),
        dma((max(mp - 1, 1), 2)), dma((max(mp - 1, 1), 2)),
    ]
    vmem = pl.BlockSpec(memory_space=pltpu.VMEM)
    return pl.pallas_call(
        functools.partial(kernel, planes, mp, c_scale),
        out_shape=(
            jax.ShapeDtypeStruct((tokens, HEADS * W), F32),
            jax.ShapeDtypeStruct((tokens // mp, W), F32),
            jax.ShapeDtypeStruct((tokens // mp, W), F32),
        ),
        in_specs=[vmem] * 7,
        out_specs=(vmem,) * 3,
        scratch_shapes=scratch,
        compiler_params=pltpu.CompilerParams(
            collective_id=0, has_side_effects=True, vmem_limit_bytes=40 << 20
        ),
        cost_estimate=pl.CostEstimate(
            flops=4_000_000_000, bytes_accessed=2_000_000, transcendentals=2_500_000
        ),
    )(queries, keys, values, inputs_x, in_b, in_c, log_decay)


def solution(mesh):
    in_specs = (
        P("seq", "mp"), P("seq", "mp"), P("seq", "mp"), P("seq", "mp"),
        P("seq", None), P("seq", None), P("seq", "mp"),
    )
    out_specs = (P("seq", "mp"), P(("seq", "mp"), None), P(("seq", "mp"), None))
    return jax.shard_map(local, mesh=mesh, in_specs=in_specs, out_specs=out_specs, check_vma=False)
```

```python
import functools
import math

import jax
import jax.numpy as jnp
from jax import lax
from jax.experimental import pallas as pl
from jax.experimental.pallas import tpu as pltpu
from jax.sharding import PartitionSpec as P

W = 128
HEADS = 8
PLANE = 4
MESH = pl.DeviceIdType.MESH
F32 = jnp.float32
BF = jnp.bfloat16
LOW = -1e30
PARTS = 4
HALF = 64


def dot(a, b):
    return lax.dot_general(a, b, (((1,), (0,)), ((), ())), preferred_element_type=F32)


def dot_nt(a, b):
    return lax.dot_general(a, b, (((1,), (1,)), ((), ())), preferred_element_type=F32)


def split(v):
    hi = v.astype(BF)
    return hi, (v - hi.astype(F32)).astype(BF)


def kernel(
    planes, mp, c_scale,
    q_hbm, k_hbm, v_hbm, x_hbm, b_hbm, c_hbm, ld_hbm,
    gx_ref, gb_ref, gc_ref,
    q_ref, k_ref, v_ref, x_ref, b_ref, c_ref, ld_ref,
    kv, cum, lsend, rs, zin, zout, run, decays, part, ag_out, s_in,
    lgsend, rsb, zinb, zoutb, agb_out, g_in,
    decay, mixt, ybuf, acc, top, den, qs, dbuf, gsum, mpb,
    in_s, kv_r, col_s, x_s, core_s, diag_s,
    rs_s, rs_r, z_s, z_r, ag_s, ag_r,
    rsb_s, rsb_r, zb_s, zb_r, agb_s, agb_r,
    mp_s, mp_r,
):
    s = lax.axis_index("seq")
    m = lax.axis_index("mp")
    z = s // PLANE
    r = s % PLANE
    base = z * PLANE
    core = r % 2
    rx = (r + 2) % PLANE
    rc = r + 1 - 2 * core
    rd = (rc + 2) % PLANE
    rows = W // mp
    levels = (planes - 1).bit_length()

    barrier = pltpu.get_barrier_semaphore()
    for k in range(1, PLANE):
        pl.semaphore_signal(
            barrier, inc=1, device_id=(base + (r + k) % PLANE, m), device_id_type=MESH
        )
    for k in range(1, mp):
        pl.semaphore_signal(barrier, inc=1, device_id=(s, (m + k) % mp), device_id_type=MESH)
    for k in range(1, planes):
        to = ((z + k) % planes) * PLANE + r
        pl.semaphore_signal(barrier, inc=1, device_id=(to, m), device_id_type=MESH)

    fetches = [
        pltpu.make_async_copy(src, dst, in_s.at[n])
        for n, (src, dst) in enumerate((
            (ld_hbm, ld_ref), (b_hbm, b_ref), (x_hbm, x_ref), (k_hbm, k_ref),
            (v_hbm, v_ref), (c_hbm, c_ref), (q_hbm, q_ref),
        ))
    ]
    for fetch in fetches:
        fetch.start()

    def remote(src, dst, send, recv, to):
        return pltpu.make_async_remote_copy(
            src_ref=src, dst_ref=dst, send_sem=send, recv_sem=recv,
            device_id=to, device_id_type=MESH,
        )

    def kv_copy(zp, rr, send, to):
        return remote(kv.at[zp, rr], kv.at[zp, rr], send, kv_r.at[zp, rr], to)

    def col(k):
        return kv_copy(z, r, col_s.at[k], (lax.rem(z + k, planes) * PLANE + r, m))

    def across(zp):
        return kv_copy(zp, r, x_s.at[zp], (base + rx, m))

    def chip(zp):
        return kv_copy(zp, r, core_s.at[zp], (base + rc, m))

    def diag(zp):
        return kv_copy(zp, rx, diag_s.at[zp], (base + rc, m))

    def arrived(zp, rr):
        kv_copy(zp, rr, x_s.at[zp], (base + rc, m)).wait_recv()

    def spread(zp):
        across(zp).start()
        chip(zp).start()

    at_row = lax.broadcasted_iota(jnp.int32, (W, W), 0)
    at_col = lax.broadcasted_iota(jnp.int32, (W, W), 1)
    tri = jnp.where(at_row <= at_col, 1.0, 0.0).astype(BF)
    fetches[0].wait()
    p0 = ld_ref[...].astype(BF)
    rest = ld_ref[...] - p0.astype(F32)
    p1 = rest.astype(BF)
    p2 = (rest - p1.astype(F32)).astype(BF)
    by_row = dot(p0, tri) + dot(p1, tri) + dot(p2, tri)
    for h in range(HEADS):
        cum[h] = jnp.broadcast_to(by_row[h : h + 1, :], (W, W)).T

    fetches[1].wait()
    fetches[2].wait()
    b = b_ref[...]
    b_t = b.astype(F32).T.astype(BF)

    pl.semaphore_wait(barrier, PLANE - 1 + mp - 1 + planes - 1)

    fetches[3].wait()
    fetches[4].wait()
    v_hi, v_lo = split(v_ref[...])
    kv[z, r, :, 0:W] = k_ref[...]
    kv[z, r, :, W : 2 * W] = v_hi
    kv[z, r, :, 2 * W : 3 * W] = v_lo
    for k in range(planes - 1, 0, -1):

        @pl.when(z + k < planes)
        def _():
            col(k).start()

    def head(ref, h):
        return ref[:, h * W : (h + 1) * W]

    def owner(k):
        return (r + k) % PLANE

    def to_owner(buf, land, send, recv, k, u):
        return remote(
            buf.at[owner(k), u], land.at[r, u], send.at[k, u], recv.at[r, u], (base + owner(k), m)
        )

    def from_peer(buf, land, send, recv, k, u):
        return remote(
            buf.at[owner(k), u], land.at[owner(k), u], send.at[k, u], recv.at[owner(k), u],
            (base + owner(k), m),
        )

    forth = (lsend, rs, rs_s, rs_r)
    back = (lgsend, rsb, rsb_s, rsb_r)
    give = (ag_out, s_in, ag_s, ag_r)
    give_back = (agb_out, g_in, agb_s, agb_r)
    far_first = (2, 3, 1)

    for g in range(2):
        for k in (2, 3, 1, 0):
            o = owner(k)
            h = 2 * o + g
            total = cum[h, W - 1 : W, :]
            ending = jnp.exp(total - cum[h])
            xh = x_ref[:, pl.ds(pl.multiple_of(h * W, W), W)]
            hi, lo = split(xh.astype(F32) * ending)
            state = dot(b_t, hi) + dot(b_t, lo)
            e = jnp.broadcast_to(jnp.exp(total), (8, W))
            to = lsend if k else rs
            for half in range(2):
                u = 2 * g + half
                to[o, u, 0:HALF, :] = state[half * HALF : (half + 1) * HALF]
                to[o, u, HALF : HALF + 8, :] = e
                if k:
                    to_owner(*forth, k, u).start()

    spread(z)

    fetches[5].wait()
    fetches[6].wait()
    c = c_ref[...]
    c_t = c.astype(F32).T.astype(BF)
    cb = dot_nt(c, b) * c_scale
    cb_t = dot_nt(b, c) * c_scale
    for h in range(HEADS):
        here = cum[h]
        other = here.T
        dec = jnp.exp(jnp.where(at_row >= at_col, here - other, LOW))
        dec_t = jnp.exp(jnp.where(at_row <= at_col, other - here, LOW))
        decay[h] = dec
        hi, lo = split(dec_t * cb_t)
        mixt[0, h] = hi
        mixt[1, h] = lo
        hi, lo = split(dec * cb)
        xh = head(x_ref, h)
        ybuf[h] = dot(hi, xh) + dot(lo, xh)
        qs[h] = head(q_ref, h)

    def pass_piece(i, carry):
        zp = z - 1 - i
        arrived(zp, r)
        spread(zp)
        return carry

    def plane_ready(zp):
        arrived(zp, rx)
        diag(zp).start()
        arrived(zp, rc)
        arrived(zp, rd)

    factor = math.log2(math.e) / math.sqrt(W)

    def attend(zp, first):
        keys = kv[zp, :, :, 0:W].reshape(PLANE * W, W)
        both = kv[zp, :, :, W : 3 * W].reshape(PLANE * W, 2 * W)
        v_top = kv[zp, :, :, W : 2 * W].reshape(PLANE * W, W)
        for h in range(HEADS):
            sc = dot_nt(qs[h], keys) * factor
            if first:
                t = lax.broadcasted_iota(jnp.int32, (W, PLANE * W), 0) + r * W
                u = lax.broadcasted_iota(jnp.int32, (W, PLANE * W), 1)
                sc = jnp.where(u <= t, sc, LOW)
            new = jnp.max(sc, axis=-1, keepdims=True)
            if not first:
                old = top[h][:, 0:1]
                new = jnp.maximum(old, new)
                scale = jnp.exp2(old - new)
            wt = jnp.exp2(sc - new)
            total = jnp.sum(wt, axis=-1, keepdims=True)
            hi, lo = split(wt)
            res = dot(hi, both)
            mix = res[:, 0:W] + res[:, W:] + dot(lo, v_top)
            if first:
                acc[h] = mix
                den[h] = jnp.broadcast_to(total, (W, W))
            else:
                acc[h] = acc[h] * scale + mix
                den[h] = den[h] * scale + total
            top[h] = jnp.broadcast_to(new, (W, W))

    plane_ready(z)
    lax.fori_loop(0, z, pass_piece, 0)
    attend(z, True)

    def attend_earlier(i, carry):
        zp = z - 1 - i
        plane_ready(zp)
        attend(zp, False)
        return carry

    def e_of(j, u):
        return rs[j, u, HALF : HALF + 1, :]

    def plane_terms(u, land, order, out):
        pre = None
        for j in order:
            if pre is not None:
                out[j, u] = pre
            local = land[j, u, 0:HALF, :]
            pre = local if pre is None else e_of(j, u) * pre + local
        part[u] = pre
        run[u] = jnp.zeros((HALF, W), F32)
        decays[u] = jnp.ones((8, W), F32)

    def hop(u, level, k, up, buf, land, send, recv):
        zt = lax.rem(z + (k if up else planes - k), planes)
        return remote(
            buf.at[u], land.at[level, u], send.at[k - 1, u], recv.at[level, u],
            (zt * PLANE + r, m),
        )

    def sends_at(zz, level):
        last = lax.rem(zz, 2 ** (level + 1)) == 2**level - 1
        return jnp.logical_and(last, zz < planes - 1)

    def send_level(u, level, zz, up, chain):
        buf = chain[0]

        @pl.when(sends_at(zz, level))
        def _():
            d = e_of(0, u) * e_of(1, u) * e_of(2, u) * e_of(3, u)
            buf[u, 0:HALF, :] = d * run[u] + part[u]
            buf[u, HALF : HALF + 8, :] = d * decays[u]
            for k in range(2**level, 0, -1):

                @pl.when(zz + k < planes)
                def _():
                    hop(u, level, k, up, *chain).start()

    def take_level(u, level, zz, up, chain):
        land = chain[1]

        @pl.when(lax.rem(zz // 2**level, 2) == 1)
        def _():
            hop(u, level, 1, up, *chain).wait_recv()
            run[u] = decays[u, 0:1, :] * land[level, u, 0:HALF, :] + run[u]
            decays[u] = decays[u] * land[level, u, HALF : HALF + 8, :]

    def hand_out(u, order, giving):
        out, land = giving[0], giving[1]
        came = run[u]
        coef = None
        for j in order:
            out[j, u] = came if coef is None else coef * came + out[j, u]
            coef = e_of(j, u) if coef is None else coef * e_of(j, u)
        for k in far_first:
            to_owner(*giving, k, u).start()
        land[r, u] = out[r, u]

    up_chain = (zout, zin, z_s, z_r)
    down_chain = (zoutb, zinb, zb_s, zb_r)
    order_up = tuple(range(PLANE))
    order_down = order_up[::-1]
    zb = planes - 1 - z

    for u in range(PARTS):
        for k in far_first:
            from_peer(*forth, k, u).wait_recv()
        plane_terms(u, rs, order_up, ag_out)
        send_level(u, 0, z, True, up_chain)

    before = jnp.where(jnp.logical_and(z % 2 == 1, z < planes - 1), 0, z)
    lax.fori_loop(0, before, attend_earlier, 0)

    for u in range(PARTS):
        for level in range(levels):
            if level:
                send_level(u, level, z, True, up_chain)
            take_level(u, level, z, True, up_chain)
        hand_out(u, order_up, give)

    lax.fori_loop(before, z, attend_earlier, 0)

    for g in range(2):
        for k in (0, 1, 2, 3):
            o = owner(k)
            h = 2 * o + g
            if k:
                for half in range(2):
                    from_peer(*give, k, 2 * g + half).wait_recv()
            rising = jnp.exp(cum[h])
            hi, lo = split(s_in[o, 2 * g : 2 * g + 2].reshape(W, W))
            inter = (dot(c, hi) + dot(c, lo)) * (rising * c_scale)
            d = ybuf[h] + inter - acc[h] / den[h]
            dbuf[h] = d
            hi, lo = split(d * rising)
            grad = (dot(c_t, hi) + dot(c_t, lo)) * c_scale
            to = lgsend if k else rsb
            for half in range(2):
                u = 2 * g + half
                to[o, u] = grad[half * HALF : (half + 1) * HALF]
                if k:
                    to_owner(*back, k, u).start()

    weighted = jnp.zeros((W, W), F32)
    grad_c = jnp.zeros((W, W), F32)
    for h in range(HEADS):
        d_hi, d_lo = split(dbuf[h])
        xh = head(x_ref, h)
        weighted += decay[h] * (dot_nt(d_hi, xh) + dot_nt(d_lo, xh))
        g = h % 2
        s_hi, s_lo = split(s_in[h // 2, 2 * g : 2 * g + 2].reshape(W, W))
        inter = dot_nt(d_hi, s_hi) + dot_nt(d_hi, s_lo) + dot_nt(d_lo, s_hi)
        grad_c += jnp.exp(cum[h]) * inter
        gx_ref[:, h * W : (h + 1) * W] = (
            dot(mixt[0, h], d_hi) + dot(mixt[0, h], d_lo) + dot(mixt[1, h], d_hi)
        )
    hi, lo = split(weighted)
    grad_c = (grad_c + dot(hi, b) + dot(lo, b)) * c_scale
    hi, lo = split(weighted.T)
    gsum[0] = (dot(hi, c) + dot(lo, c)) * c_scale
    gsum[1] = grad_c

    def mp_copy(k, which):
        to = (m + k) % mp
        return remote(
            gsum.at[which, pl.ds(pl.multiple_of(to * rows, 8), rows)],
            mpb.at[k - 1, which],
            mp_s.at[k - 1, which], mp_r.at[k - 1, which], (s, to),
        )

    for k in range(1, mp):
        mp_copy(k, 1).start()

    for u in range(PARTS):
        for k in far_first:
            from_peer(*back, k, u).wait_recv()
        plane_terms(u, rsb, order_down, agb_out)
        send_level(u, 0, zb, False, down_chain)

    for u in range(PARTS):
        for level in range(levels):
            if level:
                send_level(u, level, zb, False, down_chain)
            take_level(u, level, zb, False, down_chain)
        hand_out(u, order_down, give_back)

    grad_b = gsum[0]
    for g in range(2):
        for k in (0, 1, 2, 3):
            o = owner(k)
            h = 2 * o + g
            if k:
                for half in range(2):
                    from_peer(*give_back, k, 2 * g + half).wait_recv()
            ending = jnp.exp(cum[h, W - 1 : W, :] - cum[h])
            hi, lo = split(g_in[o, 2 * g : 2 * g + 2].reshape(W, W))
            lanes = pl.ds(pl.multiple_of(h * W, W), W)
            gx_ref[:, lanes] += (dot(b, hi) + dot(b, lo)) * ending
            xh = x_ref[:, lanes]
            grad_b += (dot_nt(xh, hi) + dot_nt(xh, lo)) * ending
    gsum[0] = grad_b
    for k in range(1, mp):
        mp_copy(k, 0).start()

    for k in far_first:
        for u in range(PARTS):
            for route in (forth, back, give, give_back):
                to_owner(*route, k, u).wait_send()
    for k in range(1, planes):

        @pl.when(z + k < planes)
        def _():
            col(k).wait_send()

    def sent(zp, carry):
        across(zp).wait_send()
        chip(zp).wait_send()
        diag(zp).wait_send()
        return carry

    lax.fori_loop(0, z + 1, sent, 0)

    for zz, up, chain in ((z, True, up_chain), (zb, False, down_chain)):
        for level in range(levels):

            @pl.when(sends_at(zz, level))
            def _():
                for k in range(2**level, 0, -1):

                    @pl.when(zz + k < planes)
                    def _():
                        for u in range(PARTS):
                            hop(u, level, k, up, *chain).wait_send()

    own = pl.ds(pl.multiple_of(m * rows, 8), rows)
    for which, out in ((1, gc_ref), (0, gb_ref)):
        total = gsum[which, own]
        for k in range(1, mp):
            mp_copy(k, which).wait_recv()
            total += mpb[k - 1, which]
        out[...] = total
    for which in range(2):
        for k in range(1, mp):
            mp_copy(k, which).wait_send()


def local(queries, keys, values, inputs_x, in_b, in_c, log_decay):
    tokens = queries.shape[0]
    seq = lax.axis_size("seq")
    mp = lax.axis_size("mp")
    planes = seq // PLANE
    c_scale = 0.5 / math.sqrt(W * tokens * seq)
    dma = pltpu.SemaphoreType.DMA
    levels = max((planes - 1).bit_length(), 1)
    reach = max(planes - 1, 1)
    msg = (PARTS, HALF + 8, W)
    plain = (PARTS, HALF, W)
    scratch = [
        pltpu.VMEM((tokens, HEADS * W), BF),
        pltpu.VMEM((tokens, W), BF),
        pltpu.VMEM((tokens, W), F32),
        pltpu.VMEM((tokens, HEADS * W), BF),
        pltpu.VMEM((tokens, W), BF),
        pltpu.VMEM((tokens, W), BF),
        pltpu.VMEM((HEADS, tokens), F32),
        pltpu.VMEM((planes, PLANE, W, 3 * W), BF),
        pltpu.VMEM((HEADS, W, W), F32),
        pltpu.VMEM((PLANE,) + msg, F32),
        pltpu.VMEM((PLANE,) + msg, F32),
        pltpu.VMEM((levels,) + msg, F32),
        pltpu.VMEM(msg, F32),
        pltpu.VMEM(plain, F32),
        pltpu.VMEM((PARTS, 8, W), F32),
        pltpu.VMEM(plain, F32),
        pltpu.VMEM((PLANE,) + plain, F32),
        pltpu.VMEM((PLANE,) + plain, F32),
        pltpu.VMEM((PLANE,) + plain, F32),
        pltpu.VMEM((PLANE,) + plain, F32),
        pltpu.VMEM((levels,) + msg, F32),
        pltpu.VMEM(msg, F32),
        pltpu.VMEM((PLANE,) + plain, F32),
        pltpu.VMEM((PLANE,) + plain, F32),
        pltpu.VMEM((HEADS, W, W), F32),
        pltpu.VMEM((2, HEADS, W, W), BF),
        pltpu.VMEM((HEADS, W, W), F32),
        pltpu.VMEM((HEADS, W, W), F32),
        pltpu.VMEM((HEADS, W, W), F32),
        pltpu.VMEM((HEADS, W, W), F32),
        pltpu.VMEM((HEADS, W, W), BF),
        pltpu.VMEM((HEADS, W, W), F32),
        pltpu.VMEM((2, W, W), F32),
        pltpu.VMEM((max(mp - 1, 1), 2, W // mp, W), F32),
        dma((7,)),
        dma((planes, PLANE)), dma((planes,)), dma((planes,)), dma((planes,)), dma((planes,)),
        dma((PLANE, PARTS)), dma((PLANE, PARTS)), dma((reach, PARTS)), dma((levels, PARTS)),
        dma((PLANE, PARTS)), dma((PLANE, PARTS)),
        dma((PLANE, PARTS)), dma((PLANE, PARTS)), dma((reach, PARTS)), dma((levels, PARTS)),
        dma((PLANE, PARTS)), dma((PLANE, PARTS)),
        dma((max(mp - 1, 1), 2)), dma((max(mp - 1, 1), 2)),
    ]
    vmem = pl.BlockSpec(memory_space=pltpu.VMEM)
    return pl.pallas_call(
        functools.partial(kernel, planes, mp, c_scale),
        out_shape=(
            jax.ShapeDtypeStruct((tokens, HEADS * W), F32),
            jax.ShapeDtypeStruct((tokens // mp, W), F32),
            jax.ShapeDtypeStruct((tokens // mp, W), F32),
        ),
        in_specs=[pl.BlockSpec(memory_space=pl.ANY)] * 7,
        out_specs=(vmem,) * 3,
        scratch_shapes=scratch,
        compiler_params=pltpu.CompilerParams(
            collective_id=0, has_side_effects=True, vmem_limit_bytes=56 << 20
        ),
        cost_estimate=pl.CostEstimate(
            flops=4_000_000_000, bytes_accessed=2_000_000, transcendentals=2_500_000
        ),
    )(queries, keys, values, inputs_x, in_b, in_c, log_decay.T)


def solution(mesh):
    in_specs = (
        P("seq", "mp"), P("seq", "mp"), P("seq", "mp"), P("seq", "mp"),
        P("seq", None), P("seq", None), P("seq", "mp"),
    )
    out_specs = (P("seq", "mp"), P(("seq", "mp"), None), P(("seq", "mp"), None))
    return jax.shard_map(local, mesh=mesh, in_specs=in_specs, out_specs=out_specs, check_vma=False)
```

```python
import functools
import math

import jax
import jax.numpy as jnp
from jax import lax
from jax.experimental import pallas as pl
from jax.experimental.pallas import tpu as pltpu
from jax.sharding import PartitionSpec as P

W = 128
HEADS = 8
PLANE = 4
MESH = pl.DeviceIdType.MESH
F32 = jnp.float32
BF = jnp.bfloat16
LOW = -1e30
PARTS = 4
HALF = 64
BLOCK = 4


def dot(a, b):
    return lax.dot_general(a, b, (((1,), (0,)), ((), ())), preferred_element_type=F32)


def dot_nt(a, b):
    return lax.dot_general(a, b, (((1,), (1,)), ((), ())), preferred_element_type=F32)


def side(*parts):
    return jnp.concatenate(parts, axis=1)


def stack(*parts):
    return jnp.concatenate(parts, axis=0)


def split(v):
    hi = v.astype(BF)
    return hi, (v - hi.astype(F32)).astype(BF)


def kernel(
    planes, mp, c_scale,
    q_hbm, k_hbm, v_hbm, x_hbm, b_hbm, c_hbm, ld_hbm,
    gx_ref, gb_ref, gc_ref,
    q_ref, k_ref, v_ref, x_ref, b_ref, c_ref, ld_ref,
    kv, cum, lsend, rs, zin, zout, run, decays, part, ag_out, s_in,
    lgsend, rsb, zinb, zoutb, agb_out, g_in,
    decay, mixt, ybuf, acc, top, den, qs, dbuf, gsum, mpb,
    in_s, kv_r, col_s, x_s, core_s, diag_s,
    rs_s, rs_r, z_s, z_r, ag_s, ag_r,
    rsb_s, rsb_r, zb_s, zb_r, agb_s, agb_r,
    mp_s, mp_r,
):
    s = lax.axis_index("seq")
    m = lax.axis_index("mp")
    z = s // PLANE
    r = s % PLANE
    base = z * PLANE
    core = r % 2
    rx = (r + 2) % PLANE
    rc = r + 1 - 2 * core
    rd = (rc + 2) % PLANE
    rows = W // mp
    levels = (planes - 1).bit_length()

    barrier = pltpu.get_barrier_semaphore()
    for k in range(1, PLANE):
        pl.semaphore_signal(
            barrier, inc=1, device_id=(base + (r + k) % PLANE, m), device_id_type=MESH
        )
    for k in range(1, mp):
        pl.semaphore_signal(barrier, inc=1, device_id=(s, (m + k) % mp), device_id_type=MESH)
    for k in range(1, planes):
        to = ((z + k) % planes) * PLANE + r
        pl.semaphore_signal(barrier, inc=1, device_id=(to, m), device_id_type=MESH)

    fetches = [
        pltpu.make_async_copy(src, dst, in_s.at[n])
        for n, (src, dst) in enumerate((
            (ld_hbm, ld_ref), (b_hbm, b_ref), (x_hbm, x_ref), (k_hbm, k_ref),
            (v_hbm, v_ref), (c_hbm, c_ref), (q_hbm, q_ref),
        ))
    ]
    for fetch in fetches:
        fetch.start()

    def remote(src, dst, send, recv, to):
        return pltpu.make_async_remote_copy(
            src_ref=src, dst_ref=dst, send_sem=send, recv_sem=recv,
            device_id=to, device_id_type=MESH,
        )

    def kv_copy(zp, rr, send, to):
        return remote(kv.at[zp, rr], kv.at[zp, rr], send, kv_r.at[zp, rr], to)

    def col(k):
        return kv_copy(z, r, col_s.at[k], (lax.rem(z + k, planes) * PLANE + r, m))

    def across(zp):
        return kv_copy(zp, r, x_s.at[zp], (base + rx, m))

    def chip(zp):
        return kv_copy(zp, r, core_s.at[zp], (base + rc, m))

    def diag(zp):
        return kv_copy(zp, rx, diag_s.at[zp], (base + rc, m))

    def arrived(zp, rr):
        kv_copy(zp, rr, x_s.at[zp], (base + rc, m)).wait_recv()

    def spread(zp):
        across(zp).start()
        chip(zp).start()

    at_row = lax.broadcasted_iota(jnp.int32, (W, W), 0)
    at_col = lax.broadcasted_iota(jnp.int32, (W, W), 1)
    tri = jnp.where(at_row <= at_col, 1.0, 0.0).astype(BF)
    fetches[0].wait()
    p0 = ld_ref[...].astype(BF)
    rest = ld_ref[...] - p0.astype(F32)
    p1 = rest.astype(BF)
    p2 = (rest - p1.astype(F32)).astype(BF)
    by_row = dot(p0, tri) + dot(p1, tri) + dot(p2, tri)
    for h in range(HEADS):
        cum[h] = jnp.broadcast_to(by_row[h : h + 1, :], (W, W)).T

    fetches[1].wait()
    fetches[2].wait()
    b = b_ref[...]
    b_t = b.astype(F32).T.astype(BF)

    pl.semaphore_wait(barrier, PLANE - 1 + mp - 1 + planes - 1)

    fetches[3].wait()
    fetches[4].wait()
    v_hi, v_lo = split(v_ref[...])
    kv[z, r, :, 0:W] = k_ref[...]
    kv[z, r, :, W : 2 * W] = v_hi
    kv[z, r, :, 2 * W : 3 * W] = v_lo
    for k in range(planes - 1, 0, -1):

        @pl.when(z + k < planes)
        def _():
            col(k).start()

    def head(ref, h):
        return ref[:, h * W : (h + 1) * W]

    def owner(k):
        return (r + k) % PLANE

    def to_owner(buf, land, send, recv, k, u):
        return remote(
            buf.at[owner(k), u], land.at[r, u], send.at[k, u], recv.at[r, u], (base + owner(k), m)
        )

    def from_peer(buf, land, send, recv, k, u):
        return remote(
            buf.at[owner(k), u], land.at[owner(k), u], send.at[k, u], recv.at[owner(k), u],
            (base + owner(k), m),
        )

    forth = (lsend, rs, rs_s, rs_r)
    back = (lgsend, rsb, rsb_s, rsb_r)
    give = (ag_out, s_in, ag_s, ag_r)
    give_back = (agb_out, g_in, agb_s, agb_r)
    far_first = (2, 3, 1)

    bb_t = side(b_t, b_t)
    for g in range(2):
        for o in range(PLANE):
            h = 2 * o + g
            total = cum[h, W - 1 : W, :]
            ending = jnp.exp(total - cum[h])
            state = dot(bb_t, stack(*split(head(x_ref, h).astype(F32) * ending)))
            e = jnp.broadcast_to(jnp.exp(total), (8, W))
            for half in range(2):
                u = 2 * g + half
                lsend[o, u, 0:HALF, :] = state[half * HALF : (half + 1) * HALF]
                lsend[o, u, HALF : HALF + 8, :] = e
        for u in (2 * g, 2 * g + 1):
            for k in far_first:
                to_owner(*forth, k, u).start()
            rs[r, u] = lsend[r, u]

    spread(z)

    fetches[5].wait()
    fetches[6].wait()
    c = c_ref[...]
    c_t = c.astype(F32).T.astype(BF)
    cb = dot_nt(c, b) * c_scale
    cb_t = dot_nt(b, c) * c_scale
    for h in range(HEADS):
        here = cum[h]
        other = jnp.broadcast_to(by_row[h : h + 1, :], (W, W))
        dec = jnp.exp(jnp.where(at_row >= at_col, here - other, LOW))
        dec_t = jnp.exp(jnp.where(at_row <= at_col, other - here, LOW))
        decay[h] = dec
        hi, lo = split(dec_t * cb_t)
        mixt[h] = side(hi, hi, lo)
        xh = head(x_ref, h)
        ybuf[h] = dot(side(*split(dec * cb)), stack(xh, xh))
        qs[h * W : (h + 1) * W, :] = head(q_ref, h)

    def pass_piece(i, carry):
        zp = z - 1 - i
        arrived(zp, r)
        spread(zp)
        return carry

    def plane_ready(zp):
        arrived(zp, rx)
        diag(zp).start()
        arrived(zp, rc)
        arrived(zp, rd)

    factor = math.log2(math.e) / math.sqrt(W)

    def attend(zp, first):
        keys = kv[zp, :, :, 0:W].reshape(PLANE * W, W)
        both = kv[zp, :, :, W : 3 * W].reshape(PLANE * W, 2 * W)
        v_top = kv[zp, :, :, W : 2 * W].reshape(PLANE * W, W)
        block = BLOCK * W
        for at in range(0, HEADS * W, block):
            sc = dot_nt(qs[at : at + block, :], keys) * factor
            if first:
                t = lax.broadcasted_iota(jnp.int32, (block, PLANE * W), 0) % W + r * W
                u = lax.broadcasted_iota(jnp.int32, (block, PLANE * W), 1)
                sc = jnp.where(u <= t, sc, LOW)
            new = jnp.broadcast_to(jnp.max(sc, axis=-1, keepdims=True), (block, W))
            if not first:
                old = top[at : at + block, :]
                new = jnp.maximum(old, new)
                scale = jnp.exp2(old - new)
            his, los, total = [], [], None
            for j in range(PLANE):
                wt = jnp.exp2(sc[:, j * W : (j + 1) * W] - new)
                total = wt if total is None else total + wt
                hi, lo = split(wt)
                his.append(hi)
                los.append(lo)
            res = dot(side(*his), both)
            mix = res[:, 0:W] + res[:, W:] + dot(side(*los), v_top)
            if not first:
                mix = acc[at : at + block, :] * scale + mix
                total = den[at : at + block, :] * scale + total
            acc[at : at + block, :] = mix
            den[at : at + block, :] = total
            top[at : at + block, :] = new

    plane_ready(z)
    lax.fori_loop(0, z, pass_piece, 0)
    attend(z, True)

    def attend_earlier(i, carry):
        zp = z - 1 - i
        plane_ready(zp)
        attend(zp, False)
        return carry

    def e_of(j, u):
        return rs[j, u, HALF : HALF + 1, :]

    def plane_terms(u, land, order, out):
        pre = None
        for j in order:
            if pre is not None:
                out[j, u] = pre
            local = land[j, u, 0:HALF, :]
            pre = local if pre is None else e_of(j, u) * pre + local
        part[u] = pre
        run[u] = jnp.zeros((HALF, W), F32)
        decays[u] = jnp.ones((8, W), F32)

    def hop(u, level, k, up, buf, land, send, recv):
        zt = lax.rem(z + (k if up else planes - k), planes)
        return remote(
            buf.at[u], land.at[level, u], send.at[k - 1, u], recv.at[level, u],
            (zt * PLANE + r, m),
        )

    def sends_at(zz, level):
        last = lax.rem(zz, 2 ** (level + 1)) == 2**level - 1
        return jnp.logical_and(last, zz < planes - 1)

    def send_level(u, level, zz, up, chain):
        buf = chain[0]

        @pl.when(sends_at(zz, level))
        def _():
            d = e_of(0, u) * e_of(1, u) * e_of(2, u) * e_of(3, u)
            buf[u, 0:HALF, :] = d * run[u] + part[u]
            buf[u, HALF : HALF + 8, :] = d * decays[u]
            for k in range(2**level, 0, -1):

                @pl.when(zz + k < planes)
                def _():
                    hop(u, level, k, up, *chain).start()

    def take_level(u, level, zz, up, chain):
        land = chain[1]

        @pl.when(lax.rem(zz // 2**level, 2) == 1)
        def _():
            hop(u, level, 1, up, *chain).wait_recv()
            run[u] = decays[u, 0:1, :] * land[level, u, 0:HALF, :] + run[u]
            decays[u] = decays[u] * land[level, u, HALF : HALF + 8, :]

    def hand_out(u, order, giving):
        out, land = giving[0], giving[1]
        came = run[u]
        coef = None
        for j in order:
            out[j, u] = came if coef is None else coef * came + out[j, u]
            coef = e_of(j, u) if coef is None else coef * e_of(j, u)
        for k in far_first:
            to_owner(*giving, k, u).start()
        land[r, u] = out[r, u]

    up_chain = (zout, zin, z_s, z_r)
    down_chain = (zoutb, zinb, zb_s, zb_r)
    order_up = tuple(range(PLANE))
    order_down = order_up[::-1]
    zb = planes - 1 - z

    for u in range(PARTS):
        for k in far_first:
            from_peer(*forth, k, u).wait_recv()
        plane_terms(u, rs, order_up, ag_out)
        send_level(u, 0, z, True, up_chain)

    before = jnp.where(jnp.logical_and(z % 2 == 1, z < planes - 1), 0, z)
    lax.fori_loop(0, before, attend_earlier, 0)

    for u in range(PARTS):
        for level in range(levels):
            if level:
                send_level(u, level, z, True, up_chain)
            take_level(u, level, z, True, up_chain)
        hand_out(u, order_up, give)

    lax.fori_loop(before, z, attend_earlier, 0)

    cc = side(c, c)
    cc_t = side(c_t, c_t)
    for g in range(2):
        for k in far_first:
            for half in range(2):
                from_peer(*give, k, 2 * g + half).wait_recv()
        for o in range(PLANE):
            h = 2 * o + g
            at = h * W
            rising = jnp.exp(cum[h])
            inter = dot(cc, stack(*split(s_in[o, 2 * g : 2 * g + 2].reshape(W, W))))
            under = jnp.sum(den[at : at + W, :], axis=-1, keepdims=True)
            d = ybuf[h] + inter * (rising * c_scale) - acc[at : at + W, :] / under
            dbuf[h] = d
            grad = dot(cc_t, stack(*split(d * rising))) * c_scale
            for half in range(2):
                lgsend[o, 2 * g + half] = grad[half * HALF : (half + 1) * HALF]
        for u in (2 * g, 2 * g + 1):
            for k in far_first:
                to_owner(*back, k, u).start()
            rsb[r, u] = lgsend[r, u]

    weighted = jnp.zeros((W, W), F32)
    grad_c = jnp.zeros((W, W), F32)
    for h in range(HEADS):
        d_hi, d_lo = split(dbuf[h])
        xh = head(x_ref, h)
        weighted += decay[h] * dot_nt(side(d_hi, d_lo), side(xh, xh))
        g = h % 2
        s_hi, s_lo = split(s_in[h // 2, 2 * g : 2 * g + 2].reshape(W, W))
        inter = dot_nt(side(d_hi, d_hi, d_lo), side(s_hi, s_lo, s_hi))
        grad_c += jnp.exp(cum[h]) * inter
        gx_ref[:, h * W : (h + 1) * W] = dot(mixt[h], stack(d_hi, d_lo, d_hi))
    grad_c = (grad_c + dot(side(*split(weighted)), stack(b, b))) * c_scale
    gsum[0] = dot(side(*split(weighted.T)), stack(c, c)) * c_scale
    gsum[1] = grad_c

    def mp_copy(k, which):
        to = (m + k) % mp
        return remote(
            gsum.at[which, pl.ds(pl.multiple_of(to * rows, 8), rows)],
            mpb.at[k - 1, which],
            mp_s.at[k - 1, which], mp_r.at[k - 1, which], (s, to),
        )

    for k in range(1, mp):
        mp_copy(k, 1).start()

    for u in range(PARTS):
        for k in far_first:
            from_peer(*back, k, u).wait_recv()
        plane_terms(u, rsb, order_down, agb_out)
        send_level(u, 0, zb, False, down_chain)

    for u in range(PARTS):
        for level in range(levels):
            if level:
                send_level(u, level, zb, False, down_chain)
            take_level(u, level, zb, False, down_chain)
        hand_out(u, order_down, give_back)

    bb = side(b, b)
    grad_b = gsum[0]
    for g in range(2):
        for k in far_first:
            for half in range(2):
                from_peer(*give_back, k, 2 * g + half).wait_recv()
        for o in range(PLANE):
            h = 2 * o + g
            ending = jnp.exp(cum[h, W - 1 : W, :] - cum[h])
            hi, lo = split(g_in[o, 2 * g : 2 * g + 2].reshape(W, W))
            gx_ref[:, h * W : (h + 1) * W] += dot(bb, stack(hi, lo)) * ending
            xh = head(x_ref, h)
            grad_b += dot_nt(side(xh, xh), side(hi, lo)) * ending
    gsum[0] = grad_b
    for k in range(1, mp):
        mp_copy(k, 0).start()

    for k in far_first:
        for u in range(PARTS):
            for route in (forth, back, give, give_back):
                to_owner(*route, k, u).wait_send()
    for k in range(1, planes):

        @pl.when(z + k < planes)
        def _():
            col(k).wait_send()

    def sent(zp, carry):
        across(zp).wait_send()
        chip(zp).wait_send()
        diag(zp).wait_send()
        return carry

    lax.fori_loop(0, z + 1, sent, 0)

    for zz, up, chain in ((z, True, up_chain), (zb, False, down_chain)):
        for level in range(levels):

            @pl.when(sends_at(zz, level))
            def _():
                for k in range(2**level, 0, -1):

                    @pl.when(zz + k < planes)
                    def _():
                        for u in range(PARTS):
                            hop(u, level, k, up, *chain).wait_send()

    own = pl.ds(pl.multiple_of(m * rows, 8), rows)
    for which, out in ((1, gc_ref), (0, gb_ref)):
        total = gsum[which, own]
        for k in range(1, mp):
            mp_copy(k, which).wait_recv()
            total += mpb[k - 1, which]
        out[...] = total
    for which in range(2):
        for k in range(1, mp):
            mp_copy(k, which).wait_send()


def local(queries, keys, values, inputs_x, in_b, in_c, log_decay):
    tokens = queries.shape[0]
    seq = lax.axis_size("seq")
    mp = lax.axis_size("mp")
    planes = seq // PLANE
    c_scale = 0.5 / math.sqrt(W * tokens * seq)
    dma = pltpu.SemaphoreType.DMA
    levels = max((planes - 1).bit_length(), 1)
    reach = max(planes - 1, 1)
    msg = (PARTS, HALF + 8, W)
    plain = (PARTS, HALF, W)
    scratch = [
        pltpu.VMEM((tokens, HEADS * W), BF),
        pltpu.VMEM((tokens, W), BF),
        pltpu.VMEM((tokens, W), F32),
        pltpu.VMEM((tokens, HEADS * W), BF),
        pltpu.VMEM((tokens, W), BF),
        pltpu.VMEM((tokens, W), BF),
        pltpu.VMEM((HEADS, tokens), F32),
        pltpu.VMEM((planes, PLANE, W, 3 * W), BF),
        pltpu.VMEM((HEADS, W, W), F32),
        pltpu.VMEM((PLANE,) + msg, F32),
        pltpu.VMEM((PLANE,) + msg, F32),
        pltpu.VMEM((levels,) + msg, F32),
        pltpu.VMEM(msg, F32),
        pltpu.VMEM(plain, F32),
        pltpu.VMEM((PARTS, 8, W), F32),
        pltpu.VMEM(plain, F32),
        pltpu.VMEM((PLANE,) + plain, F32),
        pltpu.VMEM((PLANE,) + plain, F32),
        pltpu.VMEM((PLANE,) + plain, F32),
        pltpu.VMEM((PLANE,) + plain, F32),
        pltpu.VMEM((levels,) + msg, F32),
        pltpu.VMEM(msg, F32),
        pltpu.VMEM((PLANE,) + plain, F32),
        pltpu.VMEM((PLANE,) + plain, F32),
        pltpu.VMEM((HEADS, W, W), F32),
        pltpu.VMEM((HEADS, W, 3 * W), BF),
        pltpu.VMEM((HEADS, W, W), F32),
        pltpu.VMEM((HEADS * W, W), F32),
        pltpu.VMEM((HEADS * W, W), F32),
        pltpu.VMEM((HEADS * W, W), F32),
        pltpu.VMEM((HEADS * W, W), BF),
        pltpu.VMEM((HEADS, W, W), F32),
        pltpu.VMEM((2, W, W), F32),
        pltpu.VMEM((max(mp - 1, 1), 2, W // mp, W), F32),
        dma((7,)),
        dma((planes, PLANE)), dma((planes,)), dma((planes,)), dma((planes,)), dma((planes,)),
        dma((PLANE, PARTS)), dma((PLANE, PARTS)), dma((reach, PARTS)), dma((levels, PARTS)),
        dma((PLANE, PARTS)), dma((PLANE, PARTS)),
        dma((PLANE, PARTS)), dma((PLANE, PARTS)), dma((reach, PARTS)), dma((levels, PARTS)),
        dma((PLANE, PARTS)), dma((PLANE, PARTS)),
        dma((max(mp - 1, 1), 2)), dma((max(mp - 1, 1), 2)),
    ]
    vmem = pl.BlockSpec(memory_space=pltpu.VMEM)
    return pl.pallas_call(
        functools.partial(kernel, planes, mp, c_scale),
        out_shape=(
            jax.ShapeDtypeStruct((tokens, HEADS * W), F32),
            jax.ShapeDtypeStruct((tokens // mp, W), F32),
            jax.ShapeDtypeStruct((tokens // mp, W), F32),
        ),
        in_specs=[pl.BlockSpec(memory_space=pl.ANY)] * 7,
        out_specs=(vmem,) * 3,
        scratch_shapes=scratch,
        compiler_params=pltpu.CompilerParams(
            collective_id=0, has_side_effects=True, vmem_limit_bytes=40 << 20
        ),
        cost_estimate=pl.CostEstimate(
            flops=4_000_000_000, bytes_accessed=2_000_000, transcendentals=2_500_000
        ),
    )(queries, keys, values, inputs_x, in_b, in_c, log_decay.T)


def solution(mesh):
    in_specs = (
        P("seq", "mp"), P("seq", "mp"), P("seq", "mp"), P("seq", "mp"),
        P("seq", None), P("seq", None), P("seq", "mp"),
    )
    out_specs = (P("seq", "mp"), P(("seq", "mp"), None), P(("seq", "mp"), None))
    return jax.shard_map(local, mesh=mesh, in_specs=in_specs, out_specs=out_specs, check_vma=False)
```

```python
import functools
import math

import jax
import jax.numpy as jnp
from jax import lax
from jax.experimental import pallas as pl
from jax.experimental.pallas import tpu as pltpu
from jax.sharding import PartitionSpec as P

W = 128
HEADS = 8
PLANE = 4
MESH = pl.DeviceIdType.MESH
F32 = jnp.float32
BF = jnp.bfloat16
LOW = -1e30
PARTS = 4
HALF = 64
BLOCK = 4


def dot(a, b):
    return lax.dot_general(a, b, (((1,), (0,)), ((), ())), preferred_element_type=F32)


def dot_nt(a, b):
    return lax.dot_general(a, b, (((1,), (1,)), ((), ())), preferred_element_type=F32)


def side(*parts):
    return jnp.concatenate(parts, axis=1)


def stack(*parts):
    return jnp.concatenate(parts, axis=0)


def split(v):
    hi = v.astype(BF)
    return hi, (v - hi.astype(F32)).astype(BF)


def kernel(
    planes, mp, c_scale,
    q_hbm, k_hbm, v_hbm, x_hbm, b_hbm, c_hbm, ld_hbm,
    gx_ref, gb_ref, gc_ref,
    q_ref, k_ref, v_ref, x_ref, b_ref, c_ref, ld_ref,
    kv, cum, lsend, rs, zin, zout, run, decays, part, ag_out, s_in,
    lgsend, rsb, zinb, zoutb, agb_out, g_in,
    decay, mixt, ybuf, acc, top, den, qs, dbuf, gsum, mpb,
    in_s, kv_r, col_s, x_s, core_s, diag_s,
    rs_s, rs_r, z_s, z_r, ag_s, ag_r,
    rsb_s, rsb_r, zb_s, zb_r, agb_s, agb_r,
    mp_s, mp_r,
):
    s = lax.axis_index("seq")
    m = lax.axis_index("mp")
    z = s // PLANE
    r = s % PLANE
    base = z * PLANE
    core = r % 2
    rx = (r + 2) % PLANE
    rc = r + 1 - 2 * core
    rd = (rc + 2) % PLANE
    rows = W // mp
    levels = (planes - 1).bit_length()

    barrier = pltpu.get_barrier_semaphore()
    for k in range(1, PLANE):
        pl.semaphore_signal(
            barrier, inc=1, device_id=(base + (r + k) % PLANE, m), device_id_type=MESH
        )
    for k in range(1, mp):
        pl.semaphore_signal(barrier, inc=1, device_id=(s, (m + k) % mp), device_id_type=MESH)
    for k in range(1, planes):
        to = ((z + k) % planes) * PLANE + r
        pl.semaphore_signal(barrier, inc=1, device_id=(to, m), device_id_type=MESH)

    fetches = [
        pltpu.make_async_copy(src, dst, in_s.at[n])
        for n, (src, dst) in enumerate((
            (ld_hbm, ld_ref), (b_hbm, b_ref), (x_hbm, x_ref), (k_hbm, k_ref),
            (v_hbm, v_ref), (c_hbm, c_ref), (q_hbm, q_ref),
        ))
    ]
    for fetch in fetches:
        fetch.start()

    def remote(src, dst, send, recv, to):
        return pltpu.make_async_remote_copy(
            src_ref=src, dst_ref=dst, send_sem=send, recv_sem=recv,
            device_id=to, device_id_type=MESH,
        )

    def kv_copy(zp, rr, send, to):
        return remote(kv.at[zp, rr], kv.at[zp, rr], send, kv_r.at[zp, rr], to)

    def col(k):
        return kv_copy(z, r, col_s.at[k], (lax.rem(z + k, planes) * PLANE + r, m))

    def across(zp):
        return kv_copy(zp, r, x_s.at[zp], (base + rx, m))

    def chip(zp):
        return kv_copy(zp, r, core_s.at[zp], (base + rc, m))

    def diag(zp):
        return kv_copy(zp, rx, diag_s.at[zp], (base + rc, m))

    def arrived(zp, rr):
        kv_copy(zp, rr, x_s.at[zp], (base + rc, m)).wait_recv()

    def spread(zp):
        across(zp).start()
        chip(zp).start()

    at_row = lax.broadcasted_iota(jnp.int32, (W, W), 0)
    at_col = lax.broadcasted_iota(jnp.int32, (W, W), 1)
    tri = jnp.where(at_row <= at_col, 1.0, 0.0).astype(BF)
    fetches[0].wait()
    p0 = ld_ref[...].astype(BF)
    rest = ld_ref[...] - p0.astype(F32)
    p1 = rest.astype(BF)
    p2 = (rest - p1.astype(F32)).astype(BF)
    by_row = dot(p0, tri) + dot(p1, tri) + dot(p2, tri)
    for h in range(HEADS):
        cum[h] = jnp.broadcast_to(by_row[h : h + 1, :], (W, W)).T

    fetches[1].wait()
    fetches[2].wait()
    b = b_ref[...]
    b_t = b.astype(F32).T.astype(BF)

    pl.semaphore_wait(barrier, PLANE - 1 + mp - 1 + planes - 1)

    fetches[3].wait()
    fetches[4].wait()
    v_hi, v_lo = split(v_ref[...])
    kv[z, r, :, 0:W] = k_ref[...]
    kv[z, r, :, W : 2 * W] = v_hi
    kv[z, r, :, 2 * W : 3 * W] = v_lo
    for k in range(planes - 1, 0, -1):

        @pl.when(z + k < planes)
        def _():
            col(k).start()

    def head(ref, h):
        return ref[:, h * W : (h + 1) * W]

    def owner(k):
        return (r + k) % PLANE

    def to_owner(buf, land, send, recv, k, u):
        return remote(
            buf.at[owner(k), u], land.at[r, u], send.at[k, u], recv.at[r, u], (base + owner(k), m)
        )

    def from_peer(buf, land, send, recv, k, u):
        return remote(
            buf.at[owner(k), u], land.at[owner(k), u], send.at[k, u], recv.at[owner(k), u],
            (base + owner(k), m),
        )

    forth = (lsend, rs, rs_s, rs_r)
    back = (lgsend, rsb, rsb_s, rsb_r)
    give = (ag_out, s_in, ag_s, ag_r)
    give_back = (agb_out, g_in, agb_s, agb_r)
    far_first = (2, 3, 1)

    bb_t = side(b_t, b_t)
    for g in range(2):
        for o in range(PLANE):
            h = 2 * o + g
            total = cum[h, W - 1 : W, :]
            ending = jnp.exp(total - cum[h])
            state = dot(bb_t, stack(*split(head(x_ref, h).astype(F32) * ending)))
            e = jnp.broadcast_to(jnp.exp(total), (8, W))
            for half in range(2):
                u = 2 * g + half
                lsend[o, u, 0:HALF, :] = state[half * HALF : (half + 1) * HALF]
                lsend[o, u, HALF : HALF + 8, :] = e
        for u in (2 * g, 2 * g + 1):
            for k in far_first:
                to_owner(*forth, k, u).start()
            rs[r, u] = lsend[r, u]

    spread(z)

    fetches[5].wait()
    fetches[6].wait()
    c = c_ref[...]
    c_t = c.astype(F32).T.astype(BF)
    cb = dot_nt(c, b) * c_scale
    cb_t = dot_nt(b, c) * c_scale
    for h in range(HEADS):
        here = cum[h]
        other = jnp.broadcast_to(by_row[h : h + 1, :], (W, W))
        dec = jnp.exp(jnp.where(at_row >= at_col, here - other, LOW))
        dec_t = jnp.exp(jnp.where(at_row <= at_col, other - here, LOW))
        decay[h] = dec
        hi, lo = split(dec_t * cb_t)
        mixt[h] = side(hi, hi, lo)
        xh = head(x_ref, h)
        ybuf[h] = dot(side(*split(dec * cb)), stack(xh, xh))
        qs[h * W : (h + 1) * W, :] = head(q_ref, h)

    def pass_piece(i, carry):
        zp = z - 1 - i
        arrived(zp, r)
        spread(zp)
        return carry

    def plane_ready(zp):
        arrived(zp, rx)
        diag(zp).start()
        arrived(zp, rc)
        arrived(zp, rd)

    factor = math.log2(math.e) / math.sqrt(W)

    def attend(zp, first):
        keys = kv[zp, :, :, 0:W].reshape(PLANE * W, W)
        both = kv[zp, :, :, W : 3 * W].reshape(PLANE * W, 2 * W)
        v_top = kv[zp, :, :, W : 2 * W].reshape(PLANE * W, W)
        block = BLOCK * W
        for at in range(0, HEADS * W, block):
            sc = dot_nt(qs[at : at + block, :], keys) * factor
            if first:
                t = lax.broadcasted_iota(jnp.int32, (block, PLANE * W), 0) % W + r * W
                u = lax.broadcasted_iota(jnp.int32, (block, PLANE * W), 1)
                sc = jnp.where(u <= t, sc, LOW)
            new = jnp.broadcast_to(jnp.max(sc, axis=-1, keepdims=True), (block, W))
            if not first:
                old = top[at : at + block, :]
                new = jnp.maximum(old, new)
                scale = jnp.exp2(old - new)
            his, los, total = [], [], None
            for j in range(PLANE):
                wt = jnp.exp2(sc[:, j * W : (j + 1) * W] - new)
                total = wt if total is None else total + wt
                hi, lo = split(wt)
                his.append(hi)
                los.append(lo)
            res = dot(side(*his), both)
            mix = res[:, 0:W] + res[:, W:] + dot(side(*los), v_top)
            if not first:
                mix = acc[at : at + block, :] * scale + mix
                total = den[at : at + block, :] * scale + total
            acc[at : at + block, :] = mix
            den[at : at + block, :] = total
            top[at : at + block, :] = new

    plane_ready(z)
    lax.fori_loop(0, z, pass_piece, 0)
    attend(z, True)

    def attend_earlier(i, carry):
        zp = z - 1 - i
        plane_ready(zp)
        attend(zp, False)
        return carry

    def e_of(j, u):
        return rs[j, u, HALF : HALF + 1, :]

    def plane_terms(u, land, order, out):
        pre = None
        for j in order:
            if pre is not None:
                out[j, u] = pre
            local = land[j, u, 0:HALF, :]
            pre = local if pre is None else e_of(j, u) * pre + local
        part[u] = pre
        run[u] = jnp.zeros((HALF, W), F32)
        decays[u] = jnp.ones((8, W), F32)

    def hop(u, level, k, up, buf, land, send, recv):
        zt = lax.rem(z + (k if up else planes - k), planes)
        return remote(
            buf.at[u], land.at[level, u], send.at[k - 1, u], recv.at[level, u],
            (zt * PLANE + r, m),
        )

    def sends_at(zz, level):
        last = lax.rem(zz, 2 ** (level + 1)) == 2**level - 1
        return jnp.logical_and(last, zz < planes - 1)

    def send_level(u, level, zz, up, chain):
        buf = chain[0]

        @pl.when(sends_at(zz, level))
        def _():
            d = e_of(0, u) * e_of(1, u) * e_of(2, u) * e_of(3, u)
            buf[u, 0:HALF, :] = d * run[u] + part[u]
            buf[u, HALF : HALF + 8, :] = d * decays[u]
            for k in range(2**level, 0, -1):

                @pl.when(zz + k < planes)
                def _():
                    hop(u, level, k, up, *chain).start()

    def take_level(u, level, zz, up, chain):
        land = chain[1]

        @pl.when(lax.rem(zz // 2**level, 2) == 1)
        def _():
            hop(u, level, 1, up, *chain).wait_recv()
            run[u] = decays[u, 0:1, :] * land[level, u, 0:HALF, :] + run[u]
            decays[u] = decays[u] * land[level, u, HALF : HALF + 8, :]

    def hand_out(u, order, giving):
        out, land = giving[0], giving[1]
        came = run[u]
        coef = None
        for j in order:
            out[j, u] = came if coef is None else coef * came + out[j, u]
            coef = e_of(j, u) if coef is None else coef * e_of(j, u)
        for k in far_first:
            to_owner(*giving, k, u).start()
        land[r, u] = out[r, u]

    up_chain = (zout, zin, z_s, z_r)
    down_chain = (zoutb, zinb, zb_s, zb_r)
    order_up = tuple(range(PLANE))
    order_down = order_up[::-1]
    zb = planes - 1 - z

    for u in range(PARTS):
        for k in far_first:
            from_peer(*forth, k, u).wait_recv()
        plane_terms(u, rs, order_up, ag_out)
        send_level(u, 0, z, True, up_chain)

    before = jnp.maximum(z - 2, 0)
    lax.fori_loop(0, before, attend_earlier, 0)

    for u in range(PARTS):
        for level in range(levels):
            if level:
                send_level(u, level, z, True, up_chain)
            take_level(u, level, z, True, up_chain)
        hand_out(u, order_up, give)

    lax.fori_loop(before, z, attend_earlier, 0)

    cc = side(c, c)
    cc_t = side(c_t, c_t)
    for g in range(2):
        for k in far_first:
            for half in range(2):
                from_peer(*give, k, 2 * g + half).wait_recv()
        for o in range(PLANE):
            h = 2 * o + g
            at = h * W
            rising = jnp.exp(cum[h])
            inter = dot(cc, stack(*split(s_in[o, 2 * g : 2 * g + 2].reshape(W, W))))
            under = jnp.sum(den[at : at + W, :], axis=-1, keepdims=True)
            d = ybuf[h] + inter * (rising * c_scale) - acc[at : at + W, :] / under
            dbuf[h] = d
            grad = dot(cc_t, stack(*split(d * rising))) * c_scale
            for half in range(2):
                lgsend[o, 2 * g + half] = grad[half * HALF : (half + 1) * HALF]
        for u in (2 * g, 2 * g + 1):
            for k in far_first:
                to_owner(*back, k, u).start()
            rsb[r, u] = lgsend[r, u]

    weighted = jnp.zeros((W, W), F32)
    grad_c = jnp.zeros((W, W), F32)
    for h in range(HEADS):
        d_hi, d_lo = split(dbuf[h])
        xh = head(x_ref, h)
        weighted += decay[h] * dot_nt(side(d_hi, d_lo), side(xh, xh))
        g = h % 2
        s_hi, s_lo = split(s_in[h // 2, 2 * g : 2 * g + 2].reshape(W, W))
        inter = dot_nt(side(d_hi, d_hi, d_lo), side(s_hi, s_lo, s_hi))
        grad_c += jnp.exp(cum[h]) * inter
        gx_ref[:, h * W : (h + 1) * W] = dot(mixt[h], stack(d_hi, d_lo, d_hi))
    grad_c = (grad_c + dot(side(*split(weighted)), stack(b, b))) * c_scale
    gsum[0] = dot(side(*split(weighted.T)), stack(c, c)) * c_scale
    gsum[1] = grad_c

    def mp_copy(k, which):
        to = (m + k) % mp
        return remote(
            gsum.at[which, pl.ds(pl.multiple_of(to * rows, 8), rows)],
            mpb.at[k - 1, which],
            mp_s.at[k - 1, which], mp_r.at[k - 1, which], (s, to),
        )

    for k in range(1, mp):
        mp_copy(k, 1).start()

    for u in range(PARTS):
        for k in far_first:
            from_peer(*back, k, u).wait_recv()
        plane_terms(u, rsb, order_down, agb_out)
        send_level(u, 0, zb, False, down_chain)

    for u in range(PARTS):
        for level in range(levels):
            if level:
                send_level(u, level, zb, False, down_chain)
            take_level(u, level, zb, False, down_chain)
        hand_out(u, order_down, give_back)

    bb = side(b, b)
    grad_b = gsum[0]
    for g in range(2):
        for k in far_first:
            for half in range(2):
                from_peer(*give_back, k, 2 * g + half).wait_recv()
        for o in range(PLANE):
            h = 2 * o + g
            ending = jnp.exp(cum[h, W - 1 : W, :] - cum[h])
            hi, lo = split(g_in[o, 2 * g : 2 * g + 2].reshape(W, W))
            gx_ref[:, h * W : (h + 1) * W] += dot(bb, stack(hi, lo)) * ending
            xh = head(x_ref, h)
            grad_b += dot_nt(side(xh, xh), side(hi, lo)) * ending
    gsum[0] = grad_b
    for k in range(1, mp):
        mp_copy(k, 0).start()

    for k in far_first:
        for u in range(PARTS):
            for route in (forth, back, give, give_back):
                to_owner(*route, k, u).wait_send()
    for k in range(1, planes):

        @pl.when(z + k < planes)
        def _():
            col(k).wait_send()

    def sent(zp, carry):
        across(zp).wait_send()
        chip(zp).wait_send()
        diag(zp).wait_send()
        return carry

    lax.fori_loop(0, z + 1, sent, 0)

    for zz, up, chain in ((z, True, up_chain), (zb, False, down_chain)):
        for level in range(levels):

            @pl.when(sends_at(zz, level))
            def _():
                for k in range(2**level, 0, -1):

                    @pl.when(zz + k < planes)
                    def _():
                        for u in range(PARTS):
                            hop(u, level, k, up, *chain).wait_send()

    own = pl.ds(pl.multiple_of(m * rows, 8), rows)
    for which, out in ((1, gc_ref), (0, gb_ref)):
        total = gsum[which, own]
        for k in range(1, mp):
            mp_copy(k, which).wait_recv()
            total += mpb[k - 1, which]
        out[...] = total
    for which in range(2):
        for k in range(1, mp):
            mp_copy(k, which).wait_send()


def local(queries, keys, values, inputs_x, in_b, in_c, log_decay):
    tokens = queries.shape[0]
    seq = lax.axis_size("seq")
    mp = lax.axis_size("mp")
    planes = seq // PLANE
    c_scale = 0.5 / math.sqrt(W * tokens * seq)
    dma = pltpu.SemaphoreType.DMA
    levels = max((planes - 1).bit_length(), 1)
    reach = max(planes - 1, 1)
    msg = (PARTS, HALF + 8, W)
    plain = (PARTS, HALF, W)
    scratch = [
        pltpu.VMEM((tokens, HEADS * W), BF),
        pltpu.VMEM((tokens, W), BF),
        pltpu.VMEM((tokens, W), F32),
        pltpu.VMEM((tokens, HEADS * W), BF),
        pltpu.VMEM((tokens, W), BF),
        pltpu.VMEM((tokens, W), BF),
        pltpu.VMEM((HEADS, tokens), F32),
        pltpu.VMEM((planes, PLANE, W, 3 * W), BF),
        pltpu.VMEM((HEADS, W, W), F32),
        pltpu.VMEM((PLANE,) + msg, F32),
        pltpu.VMEM((PLANE,) + msg, F32),
        pltpu.VMEM((levels,) + msg, F32),
        pltpu.VMEM(msg, F32),
        pltpu.VMEM(plain, F32),
        pltpu.VMEM((PARTS, 8, W), F32),
        pltpu.VMEM(plain, F32),
        pltpu.VMEM((PLANE,) + plain, F32),
        pltpu.VMEM((PLANE,) + plain, F32),
        pltpu.VMEM((PLANE,) + plain, F32),
        pltpu.VMEM((PLANE,) + plain, F32),
        pltpu.VMEM((levels,) + msg, F32),
        pltpu.VMEM(msg, F32),
        pltpu.VMEM((PLANE,) + plain, F32),
        pltpu.VMEM((PLANE,) + plain, F32),
        pltpu.VMEM((HEADS, W, W), F32),
        pltpu.VMEM((HEADS, W, 3 * W), BF),
        pltpu.VMEM((HEADS, W, W), F32),
        pltpu.VMEM((HEADS * W, W), F32),
        pltpu.VMEM((HEADS * W, W), F32),
        pltpu.VMEM((HEADS * W, W), F32),
        pltpu.VMEM((HEADS * W, W), BF),
        pltpu.VMEM((HEADS, W, W), F32),
        pltpu.VMEM((2, W, W), F32),
        pltpu.VMEM((max(mp - 1, 1), 2, W // mp, W), F32),
        dma((7,)),
        dma((planes, PLANE)), dma((planes,)), dma((planes,)), dma((planes,)), dma((planes,)),
        dma((PLANE, PARTS)), dma((PLANE, PARTS)), dma((reach, PARTS)), dma((levels, PARTS)),
        dma((PLANE, PARTS)), dma((PLANE, PARTS)),
        dma((PLANE, PARTS)), dma((PLANE, PARTS)), dma((reach, PARTS)), dma((levels, PARTS)),
        dma((PLANE, PARTS)), dma((PLANE, PARTS)),
        dma((max(mp - 1, 1), 2)), dma((max(mp - 1, 1), 2)),
    ]
    vmem = pl.BlockSpec(memory_space=pltpu.VMEM)
    return pl.pallas_call(
        functools.partial(kernel, planes, mp, c_scale),
        out_shape=(
            jax.ShapeDtypeStruct((tokens, HEADS * W), F32),
            jax.ShapeDtypeStruct((tokens // mp, W), F32),
            jax.ShapeDtypeStruct((tokens // mp, W), F32),
        ),
        in_specs=[pl.BlockSpec(memory_space=pl.ANY)] * 7,
        out_specs=(vmem,) * 3,
        scratch_shapes=scratch,
        compiler_params=pltpu.CompilerParams(
            collective_id=0, has_side_effects=True, vmem_limit_bytes=56 << 20
        ),
        cost_estimate=pl.CostEstimate(
            flops=4_000_000_000, bytes_accessed=2_000_000, transcendentals=2_500_000
        ),
    )(queries, keys, values, inputs_x, in_b, in_c, log_decay.T)


def solution(mesh):
    in_specs = (
        P("seq", "mp"), P("seq", "mp"), P("seq", "mp"), P("seq", "mp"),
        P("seq", None), P("seq", None), P("seq", "mp"),
    )
    out_specs = (P("seq", "mp"), P(("seq", "mp"), None), P(("seq", "mp"), None))
    return jax.shard_map(local, mesh=mesh, in_specs=in_specs, out_specs=out_specs, check_vma=False)
```

```python
import functools
import math

import jax
import jax.numpy as jnp
from jax import lax
from jax.experimental import pallas as pl
from jax.experimental.pallas import tpu as pltpu
from jax.sharding import PartitionSpec as P

W = 128
HEADS = 8
PLANE = 4
MESH = pl.DeviceIdType.MESH
F32 = jnp.float32
BF = jnp.bfloat16
LOW = -1e30
PARTS = 4
HALF = 64
BLOCK = 4


def dot(a, b):
    return lax.dot_general(a, b, (((1,), (0,)), ((), ())), preferred_element_type=F32)


def dot_nt(a, b):
    return lax.dot_general(a, b, (((1,), (1,)), ((), ())), preferred_element_type=F32)


def side(*parts):
    return jnp.concatenate(parts, axis=1)


def stack(*parts):
    return jnp.concatenate(parts, axis=0)


def split(v):
    hi = v.astype(BF)
    return hi, (v - hi.astype(F32)).astype(BF)


def kernel(
    planes, mp, c_scale,
    q_hbm, k_hbm, v_hbm, x_hbm, b_hbm, c_hbm, ld_hbm,
    gx_ref, gb_ref, gc_ref,
    q_ref, k_ref, v_ref, x_ref, b_ref, c_ref, ld_ref,
    kv, cum, lsend, rs, zin, zout, run, decays, part, ag_out, s_in,
    lgsend, rsb, zinb, zoutb, agb_out, g_in,
    decay, mixt, ybuf, acc, top, den, qs, dbuf, gsum, mpb,
    in_s, kv_r, col_s, x_s, core_s, diag_s,
    rs_s, rs_r, z_s, z_r, ag_s, ag_r,
    rsb_s, rsb_r, zb_s, zb_r, agb_s, agb_r,
    mp_s, mp_r,
):
    s = lax.axis_index("seq")
    m = lax.axis_index("mp")
    z = s // PLANE
    r = s % PLANE
    base = z * PLANE
    core = r % 2
    rx = (r + 2) % PLANE
    rc = r + 1 - 2 * core
    rd = (rc + 2) % PLANE
    rows = W // mp
    levels = (planes - 1).bit_length()

    barrier = pltpu.get_barrier_semaphore()
    for k in range(1, PLANE):
        pl.semaphore_signal(
            barrier, inc=1, device_id=(base + (r + k) % PLANE, m), device_id_type=MESH
        )
    for k in range(1, mp):
        pl.semaphore_signal(barrier, inc=1, device_id=(s, (m + k) % mp), device_id_type=MESH)
    for k in range(1, planes):
        to = ((z + k) % planes) * PLANE + r
        pl.semaphore_signal(barrier, inc=1, device_id=(to, m), device_id_type=MESH)

    fetches = [
        pltpu.make_async_copy(src, dst, in_s.at[n])
        for n, (src, dst) in enumerate((
            (ld_hbm, ld_ref), (b_hbm, b_ref), (x_hbm, x_ref), (k_hbm, k_ref),
            (v_hbm, v_ref), (c_hbm, c_ref), (q_hbm, q_ref),
        ))
    ]
    for fetch in fetches:
        fetch.start()

    def remote(src, dst, send, recv, to):
        return pltpu.make_async_remote_copy(
            src_ref=src, dst_ref=dst, send_sem=send, recv_sem=recv,
            device_id=to, device_id_type=MESH,
        )

    def kv_copy(zp, rr, send, to):
        return remote(kv.at[zp, rr], kv.at[zp, rr], send, kv_r.at[zp, rr], to)

    def col(k):
        return kv_copy(z, r, col_s.at[k], (lax.rem(z + k, planes) * PLANE + r, m))

    def across(zp):
        return kv_copy(zp, r, x_s.at[zp], (base + rx, m))

    def chip(zp):
        return kv_copy(zp, r, core_s.at[zp], (base + rc, m))

    def diag(zp):
        return kv_copy(zp, rx, diag_s.at[zp], (base + rc, m))

    def arrived(zp, rr):
        kv_copy(zp, rr, x_s.at[zp], (base + rc, m)).wait_recv()

    def spread(zp):
        across(zp).start()
        chip(zp).start()

    at_row = lax.broadcasted_iota(jnp.int32, (W, W), 0)
    at_col = lax.broadcasted_iota(jnp.int32, (W, W), 1)
    tri = jnp.where(at_row <= at_col, 1.0, 0.0).astype(BF)
    fetches[0].wait()
    p0 = ld_ref[...].astype(BF)
    rest = ld_ref[...] - p0.astype(F32)
    p1 = rest.astype(BF)
    p2 = (rest - p1.astype(F32)).astype(BF)
    by_row = dot(p0, tri) + dot(p1, tri) + dot(p2, tri)
    for h in range(HEADS):
        cum[h] = jnp.broadcast_to(by_row[h : h + 1, :], (W, W)).T

    fetches[1].wait()
    fetches[2].wait()
    b = b_ref[...]
    b_t = b.astype(F32).T.astype(BF)

    pl.semaphore_wait(barrier, PLANE - 1 + mp - 1 + planes - 1)

    fetches[3].wait()
    fetches[4].wait()
    v_hi, v_lo = split(v_ref[...])
    kv[z, r, :, 0:W] = k_ref[...]
    kv[z, r, :, W : 2 * W] = v_hi
    kv[z, r, :, 2 * W : 3 * W] = v_lo
    for k in range(planes - 1, 0, -1):

        @pl.when(z + k < planes)
        def _():
            col(k).start()

    def head(ref, h):
        return ref[:, h * W : (h + 1) * W]

    def owner(k):
        return (r + k) % PLANE

    def to_owner(buf, land, send, recv, k, u):
        return remote(
            buf.at[owner(k), u], land.at[r, u], send.at[k, u], recv.at[r, u], (base + owner(k), m)
        )

    def from_peer(buf, land, send, recv, k, u):
        return remote(
            buf.at[owner(k), u], land.at[owner(k), u], send.at[k, u], recv.at[owner(k), u],
            (base + owner(k), m),
        )

    forth = (lsend, rs, rs_s, rs_r)
    back = (lgsend, rsb, rsb_s, rsb_r)
    give = (ag_out, s_in, ag_s, ag_r)
    give_back = (agb_out, g_in, agb_s, agb_r)
    far_first = (2, 3, 1)

    bb_t = side(b_t, b_t)
    for g in range(2):
        for o in range(PLANE):
            h = 2 * o + g
            total = cum[h, W - 1 : W, :]
            ending = jnp.exp(total - cum[h])
            state = dot(bb_t, stack(*split(head(x_ref, h).astype(F32) * ending)))
            e = jnp.broadcast_to(jnp.exp(total), (8, W))
            for half in range(2):
                u = 2 * g + half
                lsend[o, u, 0:HALF, :] = state[half * HALF : (half + 1) * HALF]
                lsend[o, u, HALF : HALF + 8, :] = e
        for u in (2 * g, 2 * g + 1):
            for k in far_first:
                to_owner(*forth, k, u).start()
            rs[r, u] = lsend[r, u]

    spread(z)

    fetches[5].wait()
    fetches[6].wait()
    c = c_ref[...]
    c_t = c.astype(F32).T.astype(BF)
    cb = dot_nt(c, b) * c_scale
    cb_t = dot_nt(b, c) * c_scale
    for h in range(HEADS):
        here = cum[h]
        other = jnp.broadcast_to(by_row[h : h + 1, :], (W, W))
        dec = jnp.exp(jnp.where(at_row >= at_col, here - other, LOW))
        dec_t = jnp.exp(jnp.where(at_row <= at_col, other - here, LOW))
        decay[h] = dec
        hi, lo = split(dec_t * cb_t)
        mixt[h] = side(hi, hi, lo)
        xh = head(x_ref, h)
        ybuf[h] = dot(side(*split(dec * cb)), stack(xh, xh))
        qs[h * W : (h + 1) * W, :] = head(q_ref, h)

    def pass_piece(i, carry):
        zp = z - 1 - i
        arrived(zp, r)
        spread(zp)
        return carry

    def plane_ready(zp):
        arrived(zp, rx)
        diag(zp).start()
        arrived(zp, rc)
        arrived(zp, rd)

    factor = math.log2(math.e) / math.sqrt(W)

    def attend(zp, first):
        keys = kv[zp, :, :, 0:W].reshape(PLANE * W, W)
        both = kv[zp, :, :, W : 3 * W].reshape(PLANE * W, 2 * W)
        v_top = kv[zp, :, :, W : 2 * W].reshape(PLANE * W, W)
        block = BLOCK * W
        for at in range(0, HEADS * W, block):
            sc = dot_nt(qs[at : at + block, :], keys) * factor
            if first:
                t = lax.broadcasted_iota(jnp.int32, (block, PLANE * W), 0) % W + r * W
                u = lax.broadcasted_iota(jnp.int32, (block, PLANE * W), 1)
                sc = jnp.where(u <= t, sc, LOW)
            new = jnp.broadcast_to(jnp.max(sc, axis=-1, keepdims=True), (block, W))
            if not first:
                old = top[at : at + block, :]
                new = jnp.maximum(old, new)
                scale = jnp.exp2(old - new)
            his, los, total = [], [], None
            for j in range(PLANE):
                wt = jnp.exp2(sc[:, j * W : (j + 1) * W] - new)
                total = wt if total is None else total + wt
                hi, lo = split(wt)
                his.append(hi)
                los.append(lo)
            res = dot(side(*his), both)
            mix = res[:, 0:W] + res[:, W:] + dot(side(*los), v_top)
            if not first:
                mix = acc[at : at + block, :] * scale + mix
                total = den[at : at + block, :] * scale + total
            acc[at : at + block, :] = mix
            den[at : at + block, :] = total
            top[at : at + block, :] = new

    plane_ready(z)
    lax.fori_loop(0, z, pass_piece, 0)
    attend(z, True)

    def attend_earlier(i, carry):
        zp = z - 1 - i
        plane_ready(zp)
        attend(zp, False)
        return carry

    def e_of(j, u):
        return rs[j, u, HALF : HALF + 1, :]

    def plane_terms(u, land, order, out):
        pre = None
        for j in order:
            if pre is not None:
                out[j, u] = pre
            local = land[j, u, 0:HALF, :]
            pre = local if pre is None else e_of(j, u) * pre + local
        part[u] = pre
        run[u] = jnp.zeros((HALF, W), F32)
        decays[u] = jnp.ones((8, W), F32)

    def hop(u, level, k, up, buf, land, send, recv):
        zt = lax.rem(z + (k if up else planes - k), planes)
        return remote(
            buf.at[u], land.at[level, u], send.at[k - 1, u], recv.at[level, u],
            (zt * PLANE + r, m),
        )

    def sends_at(zz, level):
        last = lax.rem(zz, 2 ** (level + 1)) == 2**level - 1
        return jnp.logical_and(last, zz < planes - 1)

    def send_level(u, level, zz, up, chain):
        buf = chain[0]

        @pl.when(sends_at(zz, level))
        def _():
            d = e_of(0, u) * e_of(1, u) * e_of(2, u) * e_of(3, u)
            buf[u, 0:HALF, :] = d * run[u] + part[u]
            buf[u, HALF : HALF + 8, :] = d * decays[u]
            for k in range(2**level, 0, -1):

                @pl.when(zz + k < planes)
                def _():
                    hop(u, level, k, up, *chain).start()

    def take_level(u, level, zz, up, chain):
        land = chain[1]

        @pl.when(lax.rem(zz // 2**level, 2) == 1)
        def _():
            hop(u, level, 1, up, *chain).wait_recv()
            run[u] = decays[u, 0:1, :] * land[level, u, 0:HALF, :] + run[u]
            decays[u] = decays[u] * land[level, u, HALF : HALF + 8, :]

    def hand_out(u, order, giving):
        out, land = giving[0], giving[1]
        came = run[u]
        coef = None
        for j in order:
            out[j, u] = came if coef is None else coef * came + out[j, u]
            coef = e_of(j, u) if coef is None else coef * e_of(j, u)
        for k in far_first:
            to_owner(*giving, k, u).start()
        land[r, u] = out[r, u]

    up_chain = (zout, zin, z_s, z_r)
    down_chain = (zoutb, zinb, zb_s, zb_r)
    order_up = tuple(range(PLANE))
    order_down = order_up[::-1]
    zb = planes - 1 - z

    for u in range(PARTS):
        for k in far_first:
            from_peer(*forth, k, u).wait_recv()
        plane_terms(u, rs, order_up, ag_out)
        send_level(u, 0, z, True, up_chain)

    before = jnp.maximum(z - 1, 0)
    lax.fori_loop(0, before, attend_earlier, 0)

    for u in range(PARTS):
        for level in range(levels):
            if level:
                send_level(u, level, z, True, up_chain)
            take_level(u, level, z, True, up_chain)
        hand_out(u, order_up, give)

    lax.fori_loop(before, z, attend_earlier, 0)

    cc = side(c, c)
    cc_t = side(c_t, c_t)
    for g in range(2):
        for k in far_first:
            for half in range(2):
                from_peer(*give, k, 2 * g + half).wait_recv()
        for o in range(PLANE):
            h = 2 * o + g
            at = h * W
            rising = jnp.exp(cum[h])
            inter = dot(cc, stack(*split(s_in[o, 2 * g : 2 * g + 2].reshape(W, W))))
            under = jnp.sum(den[at : at + W, :], axis=-1, keepdims=True)
            d = ybuf[h] + inter * (rising * c_scale) - acc[at : at + W, :] / under
            dbuf[h] = d
            grad = dot(cc_t, stack(*split(d * rising))) * c_scale
            for half in range(2):
                lgsend[o, 2 * g + half] = grad[half * HALF : (half + 1) * HALF]
        for u in (2 * g, 2 * g + 1):
            for k in far_first:
                to_owner(*back, k, u).start()
            rsb[r, u] = lgsend[r, u]

    weighted = jnp.zeros((W, W), F32)
    grad_c = jnp.zeros((W, W), F32)
    for h in range(HEADS):
        d_hi, d_lo = split(dbuf[h])
        xh = head(x_ref, h)
        weighted += decay[h] * dot_nt(side(d_hi, d_lo), side(xh, xh))
        g = h % 2
        s_hi, s_lo = split(s_in[h // 2, 2 * g : 2 * g + 2].reshape(W, W))
        inter = dot_nt(side(d_hi, d_hi, d_lo), side(s_hi, s_lo, s_hi))
        grad_c += jnp.exp(cum[h]) * inter
        gx_ref[:, h * W : (h + 1) * W] = dot(mixt[h], stack(d_hi, d_lo, d_hi))
    grad_c = (grad_c + dot(side(*split(weighted)), stack(b, b))) * c_scale
    gsum[0] = dot(side(*split(weighted.T)), stack(c, c)) * c_scale
    gsum[1] = grad_c

    def mp_copy(k, which):
        to = (m + k) % mp
        return remote(
            gsum.at[which, pl.ds(pl.multiple_of(to * rows, 8), rows)],
            mpb.at[k - 1, which],
            mp_s.at[k - 1, which], mp_r.at[k - 1, which], (s, to),
        )

    for k in range(1, mp):
        mp_copy(k, 1).start()

    for u in range(PARTS):
        for k in far_first:
            from_peer(*back, k, u).wait_recv()
        plane_terms(u, rsb, order_down, agb_out)
        send_level(u, 0, zb, False, down_chain)

    for u in range(PARTS):
        for level in range(levels):
            if level:
                send_level(u, level, zb, False, down_chain)
            take_level(u, level, zb, False, down_chain)
        hand_out(u, order_down, give_back)

    bb = side(b, b)
    grad_b = gsum[0]
    for g in range(2):
        for k in far_first:
            for half in range(2):
                from_peer(*give_back, k, 2 * g + half).wait_recv()
        for o in range(PLANE):
            h = 2 * o + g
            ending = jnp.exp(cum[h, W - 1 : W, :] - cum[h])
            hi, lo = split(g_in[o, 2 * g : 2 * g + 2].reshape(W, W))
            gx_ref[:, h * W : (h + 1) * W] += dot(bb, stack(hi, lo)) * ending
            xh = head(x_ref, h)
            grad_b += dot_nt(side(xh, xh), side(hi, lo)) * ending
    gsum[0] = grad_b
    for k in range(1, mp):
        mp_copy(k, 0).start()

    for k in far_first:
        for u in range(PARTS):
            for route in (forth, back, give, give_back):
                to_owner(*route, k, u).wait_send()
    for k in range(1, planes):

        @pl.when(z + k < planes)
        def _():
            col(k).wait_send()

    def sent(zp, carry):
        across(zp).wait_send()
        chip(zp).wait_send()
        diag(zp).wait_send()
        return carry

    lax.fori_loop(0, z + 1, sent, 0)

    for zz, up, chain in ((z, True, up_chain), (zb, False, down_chain)):
        for level in range(levels):

            @pl.when(sends_at(zz, level))
            def _():
                for k in range(2**level, 0, -1):

                    @pl.when(zz + k < planes)
                    def _():
                        for u in range(PARTS):
                            hop(u, level, k, up, *chain).wait_send()

    own = pl.ds(pl.multiple_of(m * rows, 8), rows)
    for which, out in ((1, gc_ref), (0, gb_ref)):
        total = gsum[which, own]
        for k in range(1, mp):
            mp_copy(k, which).wait_recv()
            total += mpb[k - 1, which]
        out[...] = total
    for which in range(2):
        for k in range(1, mp):
            mp_copy(k, which).wait_send()


def local(queries, keys, values, inputs_x, in_b, in_c, log_decay):
    tokens = queries.shape[0]
    seq = lax.axis_size("seq")
    mp = lax.axis_size("mp")
    planes = seq // PLANE
    c_scale = 0.5 / math.sqrt(W * tokens * seq)
    dma = pltpu.SemaphoreType.DMA
    levels = max((planes - 1).bit_length(), 1)
    reach = max(planes - 1, 1)
    msg = (PARTS, HALF + 8, W)
    plain = (PARTS, HALF, W)
    scratch = [
        pltpu.VMEM((tokens, HEADS * W), BF),
        pltpu.VMEM((tokens, W), BF),
        pltpu.VMEM((tokens, W), F32),
        pltpu.VMEM((tokens, HEADS * W), BF),
        pltpu.VMEM((tokens, W), BF),
        pltpu.VMEM((tokens, W), BF),
        pltpu.VMEM((HEADS, tokens), F32),
        pltpu.VMEM((planes, PLANE, W, 3 * W), BF),
        pltpu.VMEM((HEADS, W, W), F32),
        pltpu.VMEM((PLANE,) + msg, F32),
        pltpu.VMEM((PLANE,) + msg, F32),
        pltpu.VMEM((levels,) + msg, F32),
        pltpu.VMEM(msg, F32),
        pltpu.VMEM(plain, F32),
        pltpu.VMEM((PARTS, 8, W), F32),
        pltpu.VMEM(plain, F32),
        pltpu.VMEM((PLANE,) + plain, F32),
        pltpu.VMEM((PLANE,) + plain, F32),
        pltpu.VMEM((PLANE,) + plain, F32),
        pltpu.VMEM((PLANE,) + plain, F32),
        pltpu.VMEM((levels,) + msg, F32),
        pltpu.VMEM(msg, F32),
        pltpu.VMEM((PLANE,) + plain, F32),
        pltpu.VMEM((PLANE,) + plain, F32),
        pltpu.VMEM((HEADS, W, W), F32),
        pltpu.VMEM((HEADS, W, 3 * W), BF),
        pltpu.VMEM((HEADS, W, W), F32),
        pltpu.VMEM((HEADS * W, W), F32),
        pltpu.VMEM((HEADS * W, W), F32),
        pltpu.VMEM((HEADS * W, W), F32),
        pltpu.VMEM((HEADS * W, W), BF),
        pltpu.VMEM((HEADS, W, W), F32),
        pltpu.VMEM((2, W, W), F32),
        pltpu.VMEM((max(mp - 1, 1), 2, W // mp, W), F32),
        dma((7,)),
        dma((planes, PLANE)), dma((planes,)), dma((planes,)), dma((planes,)), dma((planes,)),
        dma((PLANE, PARTS)), dma((PLANE, PARTS)), dma((reach, PARTS)), dma((levels, PARTS)),
        dma((PLANE, PARTS)), dma((PLANE, PARTS)),
        dma((PLANE, PARTS)), dma((PLANE, PARTS)), dma((reach, PARTS)), dma((levels, PARTS)),
        dma((PLANE, PARTS)), dma((PLANE, PARTS)),
        dma((max(mp - 1, 1), 2)), dma((max(mp - 1, 1), 2)),
    ]
    vmem = pl.BlockSpec(memory_space=pltpu.VMEM)
    return pl.pallas_call(
        functools.partial(kernel, planes, mp, c_scale),
        out_shape=(
            jax.ShapeDtypeStruct((tokens, HEADS * W), F32),
            jax.ShapeDtypeStruct((tokens // mp, W), F32),
            jax.ShapeDtypeStruct((tokens // mp, W), F32),
        ),
        in_specs=[pl.BlockSpec(memory_space=pl.ANY)] * 7,
        out_specs=(vmem,) * 3,
        scratch_shapes=scratch,
        compiler_params=pltpu.CompilerParams(
            collective_id=0, has_side_effects=True, vmem_limit_bytes=56 << 20
        ),
        cost_estimate=pl.CostEstimate(
            flops=4_000_000_000, bytes_accessed=2_000_000, transcendentals=2_500_000
        ),
    )(queries, keys, values, inputs_x, in_b, in_c, log_decay.T)


def solution(mesh):
    in_specs = (
        P("seq", "mp"), P("seq", "mp"), P("seq", "mp"), P("seq", "mp"),
        P("seq", None), P("seq", None), P("seq", "mp"),
    )
    out_specs = (P("seq", "mp"), P(("seq", "mp"), None), P(("seq", "mp"), None))
    return jax.shard_map(local, mesh=mesh, in_specs=in_specs, out_specs=out_specs, check_vma=False)
```
